32 devices in a mesh: de: 8 (over z, x), tp: 4 (over y, core).
Axes of the slice: x: 2, y: 2, z: 4, core: 2. Of those that a mesh axis runs over, the one named last changes fastest.
Arguments:
- raw_tiles: bfloat16 [4, 128, 512], P(None, ('de', 'tp')), may hold values from -6 to 6
- stem_weight: bfloat16 [48, 4, 3, 3], replicated, may hold values from -1 to 1
- embed_weight: bfloat16 [768, 1024], replicated, may hold values from -0.21875 to 0.21875
- norm_gain: float32 [1024], replicated, may hold values from 0.1 to 1.9
- router_weight: bfloat16 [1024, 8], replicated, may hold values from -0.1875 to 0.1875
- w_gate: bfloat16 [8, 1024, 4096], P('de', None, 'tp'), may hold values from -0.1875 to 0.1875
- w_up: bfloat16 [8, 1024, 4096], P('de', None, 'tp'), may hold values from -0.1875 to 0.1875
- w_down: bfloat16 [8, 4096, 1024], P('de', 'tp'), may hold values from -0.09375 to 0.09375
- routes: int32 [4096, 1], P(('de', 'tp')), may hold values from 0 to 7; in each aligned block of 128 rows (0 to 127, 128 to 255, ...) at most 32 rows name the same one
- cotangent: bfloat16 [4096, 1024], P(('de', 'tp')), may hold values from -6 to 6
Outputs:
- expert_mix: bfloat16 [4096, 1024], P(('de', 'tp'))
- grad_gate: float32 [8, 1024, 4096], P('de', None, 'tp')
- grad_up: float32 [8, 1024, 4096], P('de', None, 'tp')
- grad_down: float32 [8, 4096, 1024], P('de', 'tp')
- grad_router: float32 [1024, 8], replicated
- grad_gain: float32 [1024], replicated
- grad_embed: float32 [768, 1024], replicated
- grad_stem: float32 [48, 4, 3, 3], replicated
The draws below stay inside these ranges and needn't reach their ends.
Inputs may be any that keep to these rules, and one draw needn't show every extreme that they name: `routes`: within the tokens of one tile no expert is named more than 32 times, and in every draw some expert is named exactly 32 times in some tile.
All inputs are finite; a program needn't handle non-finite values.
Results may differ from the reference program's by a relative error of at most 0.0092.
Values may be sent and summed in bfloat16 or wider, within the bound.
A program may use at most 128 MiB of HBM per device.

```python
import math
import jax
import jax.numpy as jnp
import numpy as np
from jax import lax

D = 1024
FF = 4096
STEM_CH = 48
PATCH = 4
TOP = 1
EXP_DEV = 1
TOK_DEV = 128
EXPERTS = 8
CAP = 32
TOKENS = 4096
ROWS = 128
COLS = 512
PATCH_DIM = 768
N_DE = 8
N_TP = 4


def shard_levels(stream_key, extent, cuts, low, largest):
    factor_of, own = 1.0, jax.random.fold_in(stream_key, 6)
    for position, blocks in cuts:
        heights = jnp.exp(jax.random.uniform(jax.random.fold_in(own, position), (blocks,), jnp.float32, low / len(cuts), largest / len(cuts)))
        factor_of = factor_of * jnp.repeat(heights, extent[position] // blocks).reshape([-1 if axis == position else 1 for axis in range(len(extent))])
    return factor_of


def assign_block(key, own, number, rows, count, top, reach, lean):
    order = jax.random.permutation(key, count)
    packed, common = load_shares(count, rows * top, reach, lean, True), load_shares(count, rows * top, reach, lean, False)
    places = jnp.arange(count)

    def named(tallies, turn):
        used = int((tallies > 0).sum())
        fixed = max(1, used // 4)
        moved = fixed + (places - fixed + turn * (used - fixed)) % max(1, count - fixed)
        return jnp.zeros((count,), jnp.int32).at[order[jnp.where(places < fixed, places, moved)]].set(jnp.asarray(tallies, jnp.int32))

    tallies = jnp.where(number % 4 == 0, named(packed, number // 4), named(common, number - number // 4 - 1))
    mixed = jax.random.permutation(jax.random.fold_in(own, 3), count)
    giver, sink = mixed[0:count // 2 * 2:2], mixed[1:count // 2 * 2:2]
    room = jnp.minimum(tallies[giver] - 1, reach - tallies[sink]) // 2
    room = jnp.where((giver == order[0]) | (sink == order[0]) | (tallies[sink] == 0), 0, jnp.maximum(room, 0))
    moved = jax.random.randint(jax.random.fold_in(own, 4), (count // 2,), 0, 1 << 20) % (room + 1)
    tallies = tallies.at[giver].add(-moved).at[sink].add(moved)
    items = jnp.searchsorted(jnp.cumsum(tallies), jnp.arange(rows * top), side="right").astype(jnp.int32)
    listing = items.reshape(top, rows).T
    listing = listing[jax.random.permutation(jax.random.fold_in(own, 1), rows)]
    turn = jax.random.randint(jax.random.fold_in(own, 2), (rows, 1), 0, top)
    return jnp.take_along_axis(listing, (jnp.arange(top)[None, :] + turn) % top, axis=1)


def load_shares(count, total, most, slope, full):
    weights = [(1 << 20) // math.isqrt(standing ** slope) + 1 for standing in range(1, count + 1)]
    largest = most if full else min(most, max(-(-total // count), total * weights[0] // sum(weights)))
    least = 1 if total - largest >= count - 1 else 0
    holding, spare = [largest] + [least] * (count - 1), total - largest - least * (count - 1)
    while spare > 0:
        candidates = [i for i in range(1, count) if holding[i] < largest] or [i for i in range(1, count) if holding[i] < most]
        mass, remaining = sum([weights[i] for i in candidates]), spare
        for i in candidates:
            extra = min(most - holding[i], max(1, remaining * weights[i] // mass), spare)
            holding[i] = holding[i] + extra
            spare = spare - extra
    return np.array(holding)


def scatter_about(own_key, shape, spread, reach, shards=(), kind=jnp.bfloat16):
    drawn = spread * jax.random.normal(own_key, shape, jnp.float32)
    if shards:
        drawn = drawn * shard_levels(own_key, shape, shards, -0.22, 0.18)
    return jnp.clip(drawn, -reach, reach).astype(kind)


def setup_inputs(seed: int = 0) -> dict:
    streams_of = jax.random.split(jax.random.key(seed), 11)
    raw_tiles = scatter_about(streams_of[0], (4, ROWS, COLS), 1.0, 6.0, ((1, 32),))
    stem_weight = scatter_about(streams_of[1], (STEM_CH, 4, 3, 3), 36 ** -0.5, 1.0)
    embed_weight = scatter_about(streams_of[2], (PATCH_DIM, D), PATCH_DIM ** -0.5, 0.21875)
    norm_gain = jnp.clip(1.0 + 0.18 * jax.random.normal(streams_of[3], (D,), jnp.float32), 0.1, 1.9)
    router_weight = scatter_about(streams_of[4], (D, EXPERTS), D ** -0.5, 0.1875)
    w_gate = scatter_about(streams_of[5], (EXPERTS, D, FF), D ** -0.5, 0.1875, ((0, 8), (2, 4)))
    w_up = scatter_about(streams_of[6], (EXPERTS, D, FF), D ** -0.5, 0.1875, ((0, 8), (2, 4)))
    w_down = scatter_about(streams_of[7], (EXPERTS, FF, D), FF ** -0.5, 0.09375, ((0, 8), (1, 4)))
    routes_keys = jax.random.split(jax.random.fold_in(streams_of[8], 1), TOKENS // TOK_DEV)
    routes_turns = jax.random.permutation(jax.random.fold_in(streams_of[8], 3), TOKENS // TOK_DEV)
    routes = jax.vmap(lambda own, number: assign_block(jax.random.fold_in(streams_of[8], 2), own, number, TOK_DEV, EXPERTS, TOP, CAP, 2))(routes_keys, routes_turns).reshape((TOKENS, TOP))
    cotangent = scatter_about(streams_of[9], (TOKENS, D), 1.0, 6.0, ((0, 32),))
    return {"raw_tiles": raw_tiles, "stem_weight": stem_weight, "embed_weight": embed_weight, "norm_gain": norm_gain, "router_weight": router_weight, "w_gate": w_gate, "w_up": w_up, "w_down": w_down, "routes": routes, "cotangent": cotangent}


GELU_C = 0.7978845608028654
GELU_A = 0.044715
EPSILON = 1e-06

def gelu_value(preact):
    tanh_v = jnp.tanh(GELU_C * (preact + GELU_A * preact * preact * preact))
    return 0.5 * preact * (1.0 + tanh_v)

def gelu_slope(preact):
    tanh_v = jnp.tanh(GELU_C * (preact + GELU_A * preact * preact * preact))
    return 0.5 * (1.0 + tanh_v) + 0.5 * preact * (1.0 - tanh_v * tanh_v) * GELU_C * (1.0 + 3.0 * GELU_A * preact * preact)

def stem_stack(padded):
    pixel_rows = padded.shape[1] - 2
    pixel_cols = padded.shape[2]
    widened = jnp.pad(padded, ((0, 0), (0, 0), (1, 1)))
    pieces = [widened[:, row_step:row_step + pixel_rows, col_step:col_step + pixel_cols] for row_step in range(3) for col_step in range(3)]
    stacked = jnp.stack(pieces, axis=1)
    return stacked.reshape(36, pixel_rows * pixel_cols)

def patchify(feature_b, pixel_rows, pixel_cols):
    channels = feature_b.shape[0]
    patch_grid = feature_b.reshape(channels, pixel_rows // PATCH, PATCH, pixel_cols // PATCH, PATCH)
    patch_grid = patch_grid.transpose(1, 3, 0, 2, 4)
    return patch_grid.reshape(pixel_rows // PATCH * (pixel_cols // PATCH), channels * PATCH * PATCH)

def unpatchify(patch_cot, pixel_rows, pixel_cols, channels):
    patch_grid = patch_cot.reshape(pixel_rows // PATCH, pixel_cols // PATCH, channels, PATCH, PATCH)
    patch_grid = patch_grid.transpose(2, 0, 3, 1, 4)
    return patch_grid.reshape(channels, pixel_rows * pixel_cols)

def front(padded, stem_weight, embed_weight, norm_gain):
    pixel_rows = padded.shape[1] - 2
    pixel_cols = padded.shape[2]
    stacked = stem_stack(padded)
    kernel = stem_weight.reshape(stem_weight.shape[0], 36)
    preact = jnp.dot(kernel, stacked, preferred_element_type=jnp.float32)
    feature_b = gelu_value(preact).astype(jnp.bfloat16)
    patches_b = patchify(feature_b, pixel_rows, pixel_cols)
    embedded = jnp.dot(patches_b, embed_weight, preferred_element_type=jnp.float32)
    inv_rms = lax.rsqrt(lax.optimization_barrier(jnp.mean(embedded * embedded, axis=-1, keepdims=True)) + EPSILON)
    hidden_b = (embedded * inv_rms * norm_gain).astype(jnp.bfloat16)
    return (stacked, preact, patches_b, embedded, inv_rms, hidden_b)

def back_front(stacked, preact, patches_b, embedded, inv_rms, norm_gain, embed_weight, upstream, pixel_rows, pixel_cols):
    normed = embedded * inv_rms
    scaled = upstream * norm_gain
    embed_in = inv_rms * (scaled - normed * lax.optimization_barrier(jnp.mean(scaled * normed, axis=-1, keepdims=True)))
    gain_part = lax.optimization_barrier(jnp.sum(upstream * normed, axis=0))
    embed_cot = embed_in.astype(jnp.bfloat16)
    embed_part = jnp.dot(patches_b.T, embed_cot, preferred_element_type=jnp.float32)
    patch_cot = jnp.dot(embed_cot, embed_weight.T, preferred_element_type=jnp.float32)
    feature_cot = unpatchify(patch_cot, pixel_rows, pixel_cols, preact.shape[0])
    preact_cot = (feature_cot * gelu_slope(preact)).astype(jnp.bfloat16)
    stem_part = jnp.dot(preact_cot, stacked.T, preferred_element_type=jnp.float32)
    return (gain_part, embed_part, stem_part)

def slot_index(route_rows, experts, capacity):
    chosen = route_rows.reshape(-1)
    onehot = (chosen[:, None] == jnp.arange(experts, dtype=jnp.int32)[None, :]).astype(jnp.int32)
    before = jnp.cumsum(onehot, axis=0) - onehot
    slot_pos = lax.optimization_barrier(jnp.sum(before * onehot, axis=1))
    return (chosen * capacity + slot_pos).astype(jnp.int32)

def gate_scores(logits, routes):
    picked = jnp.take_along_axis(logits, routes, axis=1)
    return jax.nn.sigmoid(picked)

def router_cot(score_grad, gate_score, routes, experts):
    local_grad = score_grad * gate_score * (1.0 - gate_score)
    chosen_hot = (routes[:, :, None] == jnp.arange(experts, dtype=jnp.int32)[None, None, :]).astype(jnp.float32)
    return lax.optimization_barrier(jnp.sum(chosen_hot * local_grad[:, :, None], axis=1)).astype(jnp.bfloat16)

def expert_pass(operands):
    slot_rows, slot_cots, gate_matrix, up_matrix, down_matrix = operands
    gate_proj = jnp.dot(slot_rows, gate_matrix, preferred_element_type=jnp.float32)
    up_proj = jnp.dot(slot_rows, up_matrix, preferred_element_type=jnp.float32)
    sigmoid_gate = jax.nn.sigmoid(gate_proj)
    activated = gate_proj * sigmoid_gate
    hidden_act = (activated * up_proj).astype(jnp.bfloat16)
    expert_out = jnp.dot(hidden_act, down_matrix, preferred_element_type=jnp.float32).astype(jnp.bfloat16)
    act_cot = jnp.dot(slot_cots, down_matrix.T, preferred_element_type=jnp.float32)
    gate_cot = (act_cot * up_proj * (sigmoid_gate * (1.0 + gate_proj * (1.0 - sigmoid_gate)))).astype(jnp.bfloat16)
    up_cot = (act_cot * activated).astype(jnp.bfloat16)
    grad_gate = jnp.dot(slot_rows.T, gate_cot, preferred_element_type=jnp.float32)
    grad_up = jnp.dot(slot_rows.T, up_cot, preferred_element_type=jnp.float32)
    grad_down = jnp.dot(hidden_act.T, slot_cots, preferred_element_type=jnp.float32)
    slot_cot = jnp.dot(gate_cot, gate_matrix.T, preferred_element_type=jnp.float32) + jnp.dot(up_cot, up_matrix.T, preferred_element_type=jnp.float32)
    return (expert_out, slot_cot.astype(jnp.bfloat16), grad_gate, grad_up, grad_down)

def reference(raw_tiles, stem_weight, embed_weight, norm_gain, router_weight, w_gate, w_up, w_down, routes, cotangent):
    devices = N_DE * N_TP
    experts = EXP_DEV * N_DE
    capacity = CAP
    model_width = cotangent.shape[1]
    pixel_rows = raw_tiles.shape[1]
    pixel_cols = raw_tiles.shape[2]
    padded = jnp.pad(raw_tiles, ((0, 0), (1, 1), (0, 0)))
    stacked, preact, patches_b, embedded, inv_rms, hidden_b = front(padded, stem_weight, embed_weight, norm_gain)
    logits = jnp.dot(hidden_b, router_weight, preferred_element_type=jnp.float32)
    gate_score = gate_scores(logits, routes)
    slot_flat = jax.vmap(lambda route_rows: slot_index(route_rows, experts, capacity))(routes.reshape(devices, TOK_DEV, TOP))
    hidden_pairs = jnp.repeat(hidden_b, TOP, axis=0).reshape(devices, TOK_DEV * TOP, model_width)
    cot_pairs = jnp.repeat(cotangent.astype(jnp.float32), TOP, axis=0)
    out_cot = (gate_score.reshape(-1, 1) * cot_pairs).astype(jnp.bfloat16).reshape(devices, TOK_DEV * TOP, model_width)
    device_ids = jnp.arange(devices, dtype=jnp.int32)[:, None]
    blank_slots = jnp.zeros((devices, experts * capacity, model_width), jnp.bfloat16)
    sent_rows = blank_slots.at[device_ids, slot_flat].set(hidden_pairs)
    sent_cots = blank_slots.at[device_ids, slot_flat].set(out_cot)

    def by_expert(buffer):
        return buffer.reshape(devices, experts, capacity, model_width).transpose(1, 0, 2, 3).reshape(experts, devices * capacity, model_width)

    def to_source(buffer):
        return buffer.reshape(experts, devices, capacity, model_width).transpose(1, 0, 2, 3).reshape(devices, experts * capacity, model_width)
    expert_out, slot_cot, grad_gate, grad_up, grad_down = lax.map(expert_pass, (by_expert(sent_rows), by_expert(sent_cots), w_gate, w_up, w_down))
    pick_rows = jax.vmap(lambda table, index: jnp.take(table, index, axis=0))
    out_pairs = pick_rows(to_source(expert_out), slot_flat).reshape(-1, model_width)
    cot_back = pick_rows(to_source(slot_cot), slot_flat).reshape(-1, model_width)
    out_wide = out_pairs.astype(jnp.float32)
    expert_mix = lax.optimization_barrier(jnp.sum((gate_score.reshape(-1, 1) * out_wide).reshape(-1, TOP, model_width), axis=1)).astype(jnp.bfloat16)
    score_grad = lax.optimization_barrier(jnp.sum(cot_pairs * out_wide, axis=-1)).reshape(-1, TOP)
    logit_cot = router_cot(score_grad, gate_score, routes, experts)
    grad_router = jnp.dot(hidden_b.T, logit_cot, preferred_element_type=jnp.float32)
    upstream = lax.optimization_barrier(jnp.sum(cot_back.astype(jnp.float32).reshape(-1, TOP, model_width), axis=1))
    upstream = upstream + jnp.dot(logit_cot, router_weight.T, preferred_element_type=jnp.float32)
    grad_gain, grad_embed, stem_part = back_front(stacked, preact, patches_b, embedded, inv_rms, norm_gain, embed_weight, upstream, pixel_rows, pixel_cols)
    return (expert_mix, grad_gate, grad_up, grad_down, grad_router, grad_gain, grad_embed, stem_part.reshape(stem_weight.shape))
```

```python
import functools

import jax
import jax.numpy as jnp
import numpy as np
from jax import lax
from jax.experimental import pallas as pl
from jax.experimental.pallas import tpu as pltpu
from jax.sharding import PartitionSpec as P

PATCH = 4
GELU_C = 0.7978845608028654
GELU_A = 0.044715
EPSILON = 1e-06
TAPS = 40
CLASSES = PATCH * PATCH
MESH = pl.DeviceIdType.MESH
BF = jnp.bfloat16
F32 = jnp.float32
VMEM = pl.BlockSpec(memory_space=pltpu.VMEM)
NT = (((1,), (1,)), ((), ()))
TN = (((0,), (0,)), ((), ()))


def mm(a, b, dims=(((1,), (0,)), ((), ())), precision=None):
    return lax.dot_general(a, b, dims, preferred_element_type=F32, precision=precision)


def tap_table(channels):
    side = PATCH + 2
    table = np.zeros((channels * side * side, CLASSES * TAPS), np.float32)
    for q in range(CLASSES):
        for i in range(channels):
            for a in range(3):
                for b in range(3):
                    row = (i * side + q // PATCH + a) * side + q % PATCH + b
                    table[row, q * TAPS + i * 9 + a * 3 + b] = 1.0
    return table


def windows(raw):
    axes = ("de", "tp")
    count = lax.axis_size(axes)
    forward = [(i, i + 1) for i in range(count - 1)]
    backward = [(b, a) for a, b in forward]
    low = lax.ppermute(raw[:, -1:], axes, forward)
    high = lax.ppermute(raw[:, :1], axes, backward)
    padded = jnp.concatenate([low, raw, high], axis=1)
    channels, rows, cols = padded.shape
    grid = padded.reshape(channels, rows, cols // PATCH, PATCH).transpose(2, 0, 1, 3)
    left = jnp.pad(grid[:-1, :, :, -1:], ((1, 0), (0, 0), (0, 0), (0, 0)))
    right = jnp.pad(grid[1:, :, :, :1], ((0, 1), (0, 0), (0, 0), (0, 0)))
    return jnp.concatenate([left, grid, right], axis=3).reshape(cols // PATCH, -1)


def spread_of(stem):
    return (
        lax.broadcasted_iota(jnp.int32, (stem, stem * CLASSES), 0)
        == lax.broadcasted_iota(jnp.int32, (stem, stem * CLASSES), 1) // CLASSES
    )


def front_kernel(
    win_ref, table_ref, taps_ref, embed_ref, gain_ref, router_ref, routes_ref, cot_ref,
    sent_ref, preact_ref, patches_ref, embedded_ref, inv_ref, hidden_ref, score_ref, slot_ref,
    winall_ref,
):
    tokens, width = cot_ref.shape
    experts, double, _ = sent_ref.shape
    cap = double // 2
    stem = taps_ref.shape[1]
    win_all = mm(win_ref[...], table_ref[...]).astype(BF)
    winall_ref[...] = win_all
    rep = mm(taps_ref[...], spread_of(stem).astype(BF))
    cls = lax.broadcasted_iota(jnp.int32, rep.shape, 1) % CLASSES
    kernel = jnp.concatenate([jnp.where(cls == q, rep, 0.0) for q in range(CLASSES)], axis=0)
    preact = mm(win_all, kernel.astype(BF))
    preact_ref[...] = preact
    tanh_v = jnp.tanh(GELU_C * (preact + GELU_A * preact * preact * preact))
    patches = (0.5 * preact * (1.0 + tanh_v)).astype(BF)
    patches_ref[...] = patches
    embedded = mm(patches, embed_ref[...])
    embedded_ref[...] = embedded
    inv = lax.rsqrt(jnp.mean(embedded * embedded, axis=-1, keepdims=True) + EPSILON)
    inv_ref[...] = inv
    hidden = (embedded * inv * gain_ref[...]).astype(BF)
    hidden_ref[...] = hidden
    logits = mm(hidden, router_ref[...])
    routes = routes_ref[...]
    hot = routes == lax.broadcasted_iota(jnp.int32, (tokens, experts), 1)
    score = jax.nn.sigmoid(jnp.sum(jnp.where(hot, logits, 0.0), axis=1, keepdims=True))
    score_ref[...] = score
    earlier = lax.broadcasted_iota(jnp.int32, (tokens, tokens), 1) < lax.broadcasted_iota(
        jnp.int32, (tokens, tokens), 0
    )
    before = mm(earlier.astype(BF), hot.astype(BF))
    pos = jnp.sum(jnp.where(hot, before, 0.0), axis=1, keepdims=True).astype(jnp.int32)
    slot = routes * cap + pos
    slot_ref[...] = slot
    select = (slot == lax.broadcasted_iota(jnp.int32, (tokens, experts * cap), 1)).astype(BF)
    out_cot = (score * cot_ref[...].astype(F32)).astype(BF)
    rows = mm(select, hidden, TN).reshape(experts, cap, width)
    cots = mm(select, out_cot, TN).reshape(experts, cap, width)
    sent_ref[...] = jnp.concatenate([rows, cots], axis=1).astype(BF)


def greet(devices):
    barrier = pltpu.get_barrier_semaphore()
    for device in devices:
        pl.semaphore_signal(barrier, inc=1, device_id=device, device_id_type=MESH)
    pl.semaphore_wait(barrier, len(devices))


def expert_kernel(
    sent_ref, gate_ref, up_ref, down_ref,
    ret_ref, ggate_ref, gup_ref, gdown_ref,
    wg, wu, wd, grp, part, rx1, tx2, rx2, fin, rows_all, cots_all, act_all, gcot_all, ucot_all,
    stage, load_sem, own_sem, store_sem, send_sem, recv_sem,
):
    count, members, double, width = grp.shape
    cap = double // 2
    share = wg.shape[1]
    me_e, me_t = lax.axis_index("de"), lax.axis_index("tp")
    total = count * members * cap
    batch = 256
    per = batch // (members * cap)
    steps = count // per
    loads = [
        pltpu.make_async_copy(src, dst, load_sem.at[i])
        for i, (src, dst) in enumerate(
            ((gate_ref.at[0], wg), (up_ref.at[0], wu), (down_ref.at[0], wd))
        )
    ]
    for load in loads:
        load.start()

    def remote(kind, k, src, dst, device):
        return pltpu.make_async_remote_copy(
            src_ref=src, dst_ref=dst, send_sem=send_sem.at[kind, k], recv_sem=recv_sem.at[kind, k],
            device_id=device, device_id_type=MESH,
        )

    near, far = (me_e, me_t ^ 1), (me_e, me_t ^ 2)
    a2a = lambda k: remote(0, k, sent_ref.at[me_e ^ k], grp.at[k, 0], (me_e ^ k, me_t))
    to_near = lambda k: remote(1, k, grp.at[k, 0], grp.at[k, 1], near)
    to_far = lambda k: remote(2, k, grp.at[k, 0], grp.at[k, 2], far)
    pass_near = lambda k: remote(3, k, grp.at[k, 2], grp.at[k, 3], near)
    sum_near_a = lambda k: remote(4, k, part.at[k, 1], rx1.at[k, 0], near)
    sum_near_b = lambda k: remote(5, k, part.at[k, 3], rx1.at[k, 1], near)
    sum_far = lambda k: remote(6, k, tx2.at[k], rx2.at[k], far)
    back = lambda k: remote(7, k, fin.at[k], ret_ref.at[me_e], (me_e ^ k, me_t))

    greet([(me_e ^ k, me_t) for k in range(1, count)] + [near, far])
    for k in range(1, count):
        a2a(k).start()
    own = pltpu.make_async_copy(sent_ref.at[me_e], grp.at[0, 0], own_sem)
    own.start()
    own.wait()

    def forward(p):
        for i in range(per):
            k = p * per + i

            @pl.when(k > 0)
            def _():
                a2a(k).wait_recv()

            to_far(k).start()
            to_near(k).start()

    def arrive(p):
        for i in range(per):
            k = p * per + i
            to_far(k).wait_recv()
            pass_near(k).start()
        for i in range(per):
            k = p * per + i
            to_near(k).wait_recv()
            pass_near(k).wait_recv()

    def gather(p):
        blocks = grp[pl.ds(p * per, per)]
        if cap % 16:
            blocks = blocks.astype(F32)
        rows = blocks[:, :, :cap].reshape(batch, width).astype(BF)
        cots = blocks[:, :, cap:].reshape(batch, width).astype(BF)
        at = pl.ds(pl.multiple_of(p * batch, batch), batch)
        rows_all[at, :] = rows
        cots_all[at, :] = cots

    tile = 256

    def compute(p):
        at = pl.ds(pl.multiple_of(p * batch, batch), batch)

        @pl.loop(0, share // tile)
        def _(f):
            cols = pl.ds(pl.multiple_of(f * tile, tile), tile)
            gate = mm(rows_all[at, :], wg[:, cols])
            up = mm(rows_all[at, :], wu[:, cols])
            act_cot = mm(cots_all[at, :], wd[cols, :], NT)
            sig = jax.nn.sigmoid(gate)
            activated = gate * sig
            act_all[at, cols] = (activated * up).astype(BF)
            gcot_all[at, cols] = (act_cot * up * (sig * (1.0 + gate * (1.0 - sig)))).astype(BF)
            ucot_all[at, cols] = (act_cot * activated).astype(BF)

        @pl.loop(0, width // tile)
        def _(x):
            cols = pl.ds(pl.multiple_of(x * tile, tile), tile)
            out = mm(act_all[at, :], wd[:, cols])
            back_cot = mm(gcot_all[at, :], wg[cols, :], NT) + mm(ucot_all[at, :], wu[cols, :], NT)
            both = jnp.concatenate(
                [out.reshape(per, members, cap, tile), back_cot.reshape(per, members, cap, tile)],
                axis=2,
            )
            part[pl.ds(p * per, per), :, :, cols] = both.astype(BF)

    def reduce_near(p):
        for i in range(per):
            k = p * per + i
            sum_near_a(k).wait_recv()
            sum_near_b(k).wait_recv()
            tx2[k] = (part[k, 2].astype(F32) + rx1[k, 1].astype(F32)).astype(BF)
            sum_far(k).start()

    def reduce_far(p):
        for i in range(per):
            k = p * per + i
            sum_far(k).wait_recv()
            fin[k] = (
                part[k, 0].astype(F32) + rx1[k, 0].astype(F32) + rx2[k].astype(F32)
            ).astype(BF)

            @pl.when(k > 0)
            def _():
                back(k).start()

    forward(0)
    for load in loads:
        load.wait()

    @pl.loop(0, steps)
    def _(p):
        @pl.when(p < steps - 1)
        def _():
            forward(p + 1)

        arrive(p)
        gather(p)
        compute(p)
        for i in range(per):
            k = p * per + i
            sum_near_a(k).start()
            sum_near_b(k).start()

        @pl.when(p >= 1)
        def _():
            reduce_near(p - 1)

        @pl.when(p >= 2)
        def _():
            reduce_far(p - 2)

    half = 256

    def grads(j, lhs, rhs, out_ref):
        n = width // half

        def piece(c):
            return pltpu.make_async_copy(
                stage.at[j], out_ref.at[0, pl.ds(pl.multiple_of(c * half, half), half), :],
                store_sem.at[j],
            )

        @pl.loop(0, n)
        def _(c):
            @pl.when(c > 0)
            def _():
                piece(c - 1).wait()

            at = pl.ds(pl.multiple_of(c * half, half), half)
            stage[j] = mm(lhs[:, at], rhs[...], TN)
            piece(c).start()

        return lambda: piece(n - 1).wait()

    ends = [grads(0, rows_all, gcot_all, ggate_ref)]
    reduce_near(steps - 1)
    if steps >= 2:
        reduce_far(steps - 2)
    ends.append(grads(1, rows_all, ucot_all, gup_ref))
    reduce_far(steps - 1)
    own_back = pltpu.make_async_copy(fin.at[0], ret_ref.at[me_e], own_sem)
    own_back.start()
    ends.append(grads(2, act_all, cots_all, gdown_ref))
    own_back.wait()
    for end in ends:
        end()
    for k in range(1, count):
        pltpu.make_async_remote_copy(
            src_ref=fin.at[k], dst_ref=ret_ref.at[me_e ^ k], send_sem=send_sem.at[7, k],
            recv_sem=recv_sem.at[7, k], device_id=(me_e ^ k, me_t), device_id_type=MESH,
        ).wait_recv()

    for k in range(count):
        if k:
            a2a(k).wait_send()
            back(k).wait_send()
        for copy in (to_near, to_far, pass_near, sum_near_a, sum_near_b, sum_far):
            copy(k).wait_send()


def token_kernel(
    ret_ref, slot_ref, routes_ref, score_ref, cot_ref, hidden_ref, embedded_ref, inv_ref, gain_ref,
    patches_ref, embed_ref, router_ref, preact_ref, winall_ref,
    mix_ref, big_ref, small_ref,
    eb, e_rx1, e_acc1, e_rx2, e_acc2, e_rx3, e_piece,
    sb, s_rx1, s_acc1, s_rx2, s_rx3, send_sem, recv_sem, own_sem,
):
    tokens, width = cot_ref.shape
    experts, double, _ = ret_ref.shape
    cap = double // 2
    chunks, patch_dim, lanes = eb.shape
    z_count = e_rx3.shape[0]
    piece = patch_dim // z_count
    me_e, me_t = lax.axis_index("de"), lax.axis_index("tp")
    b, g, z = me_t & 1, (me_t >> 1) * 2 + (me_e & 1), me_e >> 1
    near = (me_e, me_t ^ 1)
    cross = [None] + [(me_e ^ (r & 1), me_t ^ (r & 2)) for r in range(1, 4)]
    along = [None] + [(me_e ^ (2 * r), me_t) for r in range(1, z_count)]
    greet([near] + cross[1:] + along[1:])

    ret = ret_ref[...]
    if cap % 16:
        ret = ret.astype(F32)
    out_flat = ret[:, :cap].reshape(experts * cap, width).astype(BF)
    cot_flat = ret[:, cap:].reshape(experts * cap, width).astype(BF)
    select = (
        slot_ref[...] == lax.broadcasted_iota(jnp.int32, (tokens, experts * cap), 1)
    ).astype(BF)
    score = score_ref[...]
    out_wide = mm(select, out_flat)
    mix_ref[...] = (score * out_wide).astype(BF)
    score_grad = jnp.sum(cot_ref[...].astype(F32) * out_wide, axis=1, keepdims=True)
    local_grad = score_grad * score * (1.0 - score)
    hot = routes_ref[...] == lax.broadcasted_iota(jnp.int32, (tokens, experts), 1)
    logit_cot = jnp.where(hot, local_grad, 0.0).astype(BF)
    router_part = mm(logit_cot, hidden_ref[...], TN)
    upstream = mm(select, cot_flat) + mm(logit_cot, router_ref[...], NT)
    inv = inv_ref[...]
    normed = embedded_ref[...] * inv
    scaled = upstream * gain_ref[...]
    embed_cot = (
        inv * (scaled - normed * jnp.mean(scaled * normed, axis=1, keepdims=True))
    ).astype(BF)
    gain_part = jnp.sum(upstream * normed, axis=0, keepdims=True)
    patches = patches_ref[...]
    for c in range(0, chunks, 2):
        both = mm(patches, embed_cot[:, c * lanes : (c + 2) * lanes], TN).astype(BF)
        eb[c] = both[:, :lanes]
        eb[c + 1] = both[:, lanes:]

    def remote(kind, k, src, dst, device):
        return pltpu.make_async_remote_copy(
            src_ref=src, dst_ref=dst, send_sem=send_sem.at[kind, k], recv_sem=recv_sem.at[kind, k],
            device_id=device, device_id_type=MESH,
        )

    sent = []

    def send(*args):
        copy = remote(*args)
        copy.start()
        sent.append(copy)

    other = pl.ds((1 - b) * 4, 4)
    mine = pl.ds(b * 4, 4)
    send(0, 0, eb.at[other], e_rx1, near)

    preact = preact_ref[...]
    patch_cot = mm(embed_cot, embed_ref[...], NT)
    tanh_v = jnp.tanh(GELU_C * (preact + GELU_A * preact * preact * preact))
    slope = 0.5 * (1.0 + tanh_v) + 0.5 * preact * (1.0 - tanh_v * tanh_v) * GELU_C * (
        1.0 + 3.0 * GELU_A * preact * preact
    )
    preact_cot = (patch_cot * slope).astype(BF)
    cls = lax.broadcasted_iota(jnp.int32, (TAPS, patch_dim), 1) % CLASSES
    taps_all = mm(winall_ref[...], preact_cot, TN)
    taps = jnp.zeros((TAPS, patch_dim), F32)
    for q in range(CLASSES):
        taps = taps + jnp.where(cls == q, taps_all[q * TAPS : (q + 1) * TAPS], 0.0)
    stem = patch_dim // CLASSES
    stem_part = mm(taps, spread_of(stem).astype(F32), NT, lax.Precision.HIGHEST)
    stem_part = jnp.concatenate([stem_part, jnp.zeros((TAPS, lanes - stem), F32)], axis=1)
    gain_rows = jnp.broadcast_to(gain_part, (8, width))
    for c in range(chunks):
        at = slice(c * lanes, (c + 1) * lanes)
        sb[c, :experts] = router_part[:, at]
        sb[c, experts : experts + 8] = gain_rows[:, at]
        sb[c, experts + 8 :] = (
            stem_part[c * 8 : c * 8 + 8] if c * 8 < TAPS else jnp.zeros((8, lanes), F32)
        )
    send(1, 0, sb.at[other], s_rx1, near)

    remote(0, 0, eb.at[other], e_rx1, near).wait_recv()
    for c in range(4):
        e_acc1[c] = (eb[b * 4 + c].astype(F32) + e_rx1[c].astype(F32)).astype(BF)
    for r in range(1, 4):
        send(2, r, e_acc1.at[g ^ r], e_rx2.at[r], cross[r])
    remote(1, 0, sb.at[other], s_rx1, near).wait_recv()
    for c in range(4):
        s_acc1[c] = sb[b * 4 + c] + s_rx1[c]
    for r in range(1, 4):
        send(3, r, s_acc1.at[g ^ r], s_rx2.at[r], cross[r])
    for r in range(1, 4):
        remote(2, r, e_acc1.at[g ^ r], e_rx2.at[r], cross[r]).wait_recv()
    e_acc2[...] = (
        e_acc1[g].astype(F32) + e_rx2[1].astype(F32) + e_rx2[2].astype(F32) + e_rx2[3].astype(F32)
    ).astype(BF)
    rows_of = lambda i: pl.ds(pl.multiple_of(i * piece, piece), piece)
    for r in range(1, z_count):
        send(4, r, e_acc2.at[rows_of(z ^ r)], e_rx3.at[r], along[r])
    for r in range(1, 4):
        remote(3, r, s_acc1.at[g ^ r], s_rx2.at[r], cross[r]).wait_recv()
    s_rx3[z] = s_acc1[g] + s_rx2[1] + s_rx2[2] + s_rx2[3]
    for r in range(1, z_count):
        send(5, r, s_rx3.at[z], s_rx3.at[z], along[r])
    total = e_acc2[rows_of(z), :].astype(F32)
    for r in range(1, z_count):
        remote(4, r, e_acc2.at[rows_of(z ^ r)], e_rx3.at[r], along[r]).wait_recv()
        total = total + e_rx3[r].astype(F32)
    e_piece[...] = total.astype(BF)
    own = b * 4 + g
    for r in range(1, z_count):
        send(6, r, e_piece, big_ref.at[own, rows_of(z)], along[r])
    big_ref[own, rows_of(z), :] = total.astype(BF)
    for r in range(1, z_count):
        remote(5, r, s_rx3.at[z], s_rx3.at[z ^ r], along[r]).wait_recv()
    s_total = s_rx3[0]
    for i in range(1, z_count):
        s_total = s_total + s_rx3[i]
    small_ref[own] = s_total
    for r in range(1, 4):
        send(7, r, small_ref.at[own], small_ref.at[own], cross[r])
    for r in range(1, z_count):
        remote(6, r, e_piece, big_ref.at[own, rows_of(z ^ r)], along[r]).wait_recv()
    for r in range(1, 4):
        send(8, r, big_ref.at[own], big_ref.at[own], cross[r])
    for r in range(1, 4):
        remote(7, r, small_ref.at[own], small_ref.at[b * 4 + (g ^ r)], cross[r]).wait_recv()
    send(9, 0, small_ref.at[mine], small_ref.at[mine], near)
    send(10, 0, big_ref.at[own], big_ref.at[own], near)
    for r in range(1, 4):
        theirs = b * 4 + (g ^ r)
        remote(8, r, big_ref.at[own], big_ref.at[theirs], cross[r]).wait_recv()
        send(10, r, big_ref.at[theirs], big_ref.at[theirs], near)
    remote(9, 0, small_ref.at[mine], small_ref.at[other], near).wait_recv()
    for r in range(4):
        theirs = (1 - b) * 4 + (g ^ r)
        remote(10, r, big_ref.at[theirs], big_ref.at[theirs], near).wait_recv()
    for copy in sent:
        copy.wait_send()


def local(
    raw_tiles, stem_weight, embed_weight, norm_gain, router_weight, w_gate, w_up, w_down, routes,
    cotangent,
):
    tokens, width = cotangent.shape
    owners, members = lax.axis_size("de"), lax.axis_size("tp")
    experts = w_gate.shape[0] * owners
    cap = 2 * tokens // experts
    share = w_gate.shape[2]
    channels = raw_tiles.shape[0]
    stem = stem_weight.shape[0]
    patch_dim = embed_weight.shape[0]
    total = owners * members * cap
    shape = jax.ShapeDtypeStruct
    win = windows(raw_tiles)
    table = jnp.asarray(tap_table(channels), BF)
    taps = jnp.pad(stem_weight.reshape(stem, channels * 9).T, ((0, TAPS - channels * 9), (0, 0)))
    gain = norm_gain.reshape(1, width)
    sent, preact, patches, embedded, inv, hidden, score, slot, winall = pl.pallas_call(
        front_kernel,
        out_shape=(
            shape((experts, 2 * cap, width), BF),
            shape((tokens, patch_dim), F32),
            shape((tokens, patch_dim), BF),
            shape((tokens, width), F32),
            shape((tokens, 1), F32),
            shape((tokens, width), BF),
            shape((tokens, 1), F32),
            shape((tokens, 1), jnp.int32),
            shape((tokens, CLASSES * TAPS), BF),
        ),
        in_specs=[VMEM] * 8,
        out_specs=(VMEM,) * 9,
        compiler_params=pltpu.CompilerParams(vmem_limit_bytes=32 << 20),
        name="front",
    )(win, table, taps, embed_weight, gain, router_weight, routes, cotangent)

    anywhere = pl.BlockSpec(memory_space=pl.ANY)
    block = (2 * cap, width)
    ret, grad_gate, grad_up, grad_down = pl.pallas_call(
        expert_kernel,
        out_shape=(
            shape((experts,) + block, BF),
            shape(w_gate.shape, F32),
            shape(w_up.shape, F32),
            shape(w_down.shape, F32),
        ),
        in_specs=[VMEM] + [anywhere] * 3,
        out_specs=(VMEM,) + (anywhere,) * 3,
        scratch_shapes=[
            pltpu.VMEM((width, share), BF),
            pltpu.VMEM((width, share), BF),
            pltpu.VMEM((share, width), BF),
            pltpu.VMEM((owners, members) + block, BF),
            pltpu.VMEM((owners, members) + block, BF),
            pltpu.VMEM((owners, 2) + block, BF),
            pltpu.VMEM((owners,) + block, BF),
            pltpu.VMEM((owners,) + block, BF),
            pltpu.VMEM((owners,) + block, BF),
            pltpu.VMEM((total, width), BF),
            pltpu.VMEM((total, width), BF),
            pltpu.VMEM((total, share), BF),
            pltpu.VMEM((total, share), BF),
            pltpu.VMEM((total, share), BF),
            pltpu.VMEM((3, 256, width), F32),
            pltpu.SemaphoreType.DMA((3,)),
            pltpu.SemaphoreType.DMA,
            pltpu.SemaphoreType.DMA((3,)),
            pltpu.SemaphoreType.DMA((8, owners)),
            pltpu.SemaphoreType.DMA((8, owners)),
        ],
        compiler_params=pltpu.CompilerParams(
            vmem_limit_bytes=56 << 20, collective_id=1, has_side_effects=True
        ),
        name="experts",
    )(sent, w_gate, w_up, w_down)

    lanes = width // 8
    z_count = owners // 2
    small_rows = experts + 16
    mix, big, small = pl.pallas_call(
        token_kernel,
        out_shape=(
            shape((tokens, width), BF),
            shape((8, patch_dim, lanes), BF),
            shape((8, small_rows, lanes), F32),
        ),
        in_specs=[VMEM] * 14,
        out_specs=(VMEM,) * 3,
        scratch_shapes=[
            pltpu.VMEM((8, patch_dim, lanes), BF),
            pltpu.VMEM((4, patch_dim, lanes), BF),
            pltpu.VMEM((4, patch_dim, lanes), BF),
            pltpu.VMEM((4, patch_dim, lanes), BF),
            pltpu.VMEM((patch_dim, lanes), BF),
            pltpu.VMEM((z_count, patch_dim // z_count, lanes), BF),
            pltpu.VMEM((patch_dim // z_count, lanes), BF),
            pltpu.VMEM((8, small_rows, lanes), F32),
            pltpu.VMEM((4, small_rows, lanes), F32),
            pltpu.VMEM((4, small_rows, lanes), F32),
            pltpu.VMEM((4, small_rows, lanes), F32),
            pltpu.VMEM((z_count, small_rows, lanes), F32),
            pltpu.SemaphoreType.DMA((11, max(4, z_count))),
            pltpu.SemaphoreType.DMA((11, max(4, z_count))),
            pltpu.SemaphoreType.DMA,
        ],
        compiler_params=pltpu.CompilerParams(
            vmem_limit_bytes=40 << 20, collective_id=2, has_side_effects=True
        ),
        name="tokens",
    )(
        ret, slot, routes, score, cotangent, hidden, embedded, inv, gain, patches, embed_weight,
        router_weight, preact, winall,
    )
    grad_embed = big.transpose(1, 0, 2).reshape(patch_dim, width).astype(F32)
    grad_router = small[:, :experts].transpose(0, 2, 1).reshape(width, experts)
    grad_gain = small[:, experts].reshape(width)
    taps_grad = small[: TAPS // 8, experts + 8 :].reshape(TAPS, lanes)[: channels * 9, :stem]
    return (
        mix, grad_gate, grad_up, grad_down, grad_router, grad_gain, grad_embed,
        taps_grad.T.reshape(stem_weight.shape),
    )


def solution(mesh):
    tiles = P(("de", "tp"), None)
    columns, rows = P("de", None, "tp"), P("de", "tp", None)
    return jax.shard_map(
        local,
        mesh=mesh,
        in_specs=(
            P(None, ("de", "tp"), None), P(), P(), P(), P(), columns, columns, rows, tiles, tiles,
        ),
        out_specs=(tiles, columns, columns, rows, P(), P(), P(), P()),
        check_vma=False,
    )
```

```python
import jax
import jax.numpy as jnp
import numpy as np
from jax import lax
from jax.experimental import pallas as pl
from jax.experimental.pallas import tpu as pltpu
from jax.sharding import PartitionSpec as P

PATCH = 4
GELU_C = 0.7978845608028654
GELU_A = 0.044715
EPSILON = 1e-06
TAPS = 40
CLASSES = PATCH * PATCH
MESH = pl.DeviceIdType.MESH
BF = jnp.bfloat16
F32 = jnp.float32
VMEM = pl.BlockSpec(memory_space=pltpu.VMEM)
NT = (((1,), (1,)), ((), ()))
TN = (((0,), (0,)), ((), ()))


def mm(a, b, dims=(((1,), (0,)), ((), ())), precision=None):
    return lax.dot_general(a, b, dims, preferred_element_type=F32, precision=precision)


def tap_table(channels):
    side = PATCH + 2
    table = np.zeros((side, channels * 8, CLASSES * TAPS), np.float32)
    for q in range(CLASSES):
        for i in range(channels):
            for a in range(3):
                for b in range(3):
                    table[q % PATCH + b, i * 8 + q // PATCH + a, q * TAPS + i * 9 + a * 3 + b] = 1.0
    return table.reshape(side * channels * 8, CLASSES * TAPS)


def spread_of(stem):
    return (
        lax.broadcasted_iota(jnp.int32, (stem, stem * CLASSES), 0)
        == lax.broadcasted_iota(jnp.int32, (stem, stem * CLASSES), 1) // CLASSES
    )


def greet(devices):
    barrier = pltpu.get_barrier_semaphore()
    for device in devices:
        pl.semaphore_signal(barrier, inc=1, device_id=device, device_id_type=MESH)
    pl.semaphore_wait(barrier, len(devices))


def step_kernel(
    raw_ref, taps_ref, gain_ref, router_ref, routes_ref, cot_ref,
    table_hbm, embed_hbm, gate_ref, up_ref, down_ref,
    mix_ref, big_ref, small_ref, ggate_ref, gup_ref, gdown_ref,
    table_ref, embed_ref, wg, wu, wd, halo, sent_r, sent_c, grp_r, grp_c, part, rx1, rx2, ret_ref,
    rows_all, cots_all, act_all, gcot_all, ucot_all, stage,
    preact_ref, patches_ref, embedded_ref, inv_ref, hidden_ref, score_ref, slot_ref, winall_ref,
    eb, e_rx1, e_acc1, e_rx2, e_acc2, e_rx3, e_piece, sb, s_rx1, s_acc1, s_rx2, s_rx3,
    load_sem, own_sem, store_sem, halo_send, halo_recv, send_sem, recv_sem, red_send, red_recv,
):
    count, members, cap, width = grp_c.shape
    tokens = cot_ref.shape[0]
    experts = count
    share = wg.shape[1]
    stem = taps_ref.shape[0]
    channels, strip, pixel_cols = raw_ref.shape
    me_e, me_t = lax.axis_index("de"), lax.axis_index("tp")
    batch = 256
    per = batch // (members * cap)
    steps = count // per
    chunks, patch_dim, lanes = eb.shape
    z_count = e_rx3.shape[0]
    piece = patch_dim // z_count
    b, g, z = me_t & 1, (me_t >> 1) * 2 + (me_e & 1), me_e >> 1
    near, far = (me_e, me_t ^ 1), (me_e, me_t ^ 2)
    cross = [None] + [(me_e ^ (r & 1), me_t ^ (r & 2)) for r in range(1, 4)]
    along = [None] + [(me_e ^ (2 * r), me_t) for r in range(1, z_count)]
    loads = [
        pltpu.make_async_copy(src, dst, load_sem.at[i])
        for i, (src, dst) in enumerate(
            (
                (table_hbm, table_ref), (embed_hbm, embed_ref), (gate_ref.at[0], wg),
                (up_ref.at[0], wu), (down_ref.at[0], wd),
            )
        )
    ]
    for load in loads:
        load.start()

    def remote(kind, k, src, dst, device):
        return pltpu.make_async_remote_copy(
            src_ref=src, dst_ref=dst, send_sem=send_sem.at[kind, k], recv_sem=recv_sem.at[kind, k],
            device_id=device, device_id_type=MESH,
        )

    def moves(base, sent_ref, grp):
        return (
            lambda k: remote(base, k, sent_ref.at[me_e ^ k], grp.at[k, 0], (me_e ^ k, me_t)),
            lambda k: remote(base + 1, k, grp.at[k, 0], grp.at[k, 1], near),
            lambda k: remote(base + 2, k, grp.at[k, 0], grp.at[k, 2], far),
            lambda k: remote(base + 3, k, grp.at[k, 2], grp.at[k, 3], near),
        )

    rows_moves = moves(0, sent_r, grp_r)
    cots_moves = moves(4, sent_c, grp_c)
    sum_near_a = lambda k: remote(8, k, part.at[k, 1], rx1.at[k, 0], near)
    sum_near_b = lambda k: remote(9, k, part.at[k, 3], rx1.at[k, 1], near)
    sum_far = lambda k: remote(10, k, part.at[k, 2], rx2.at[k], far)
    back = lambda k: remote(11, k, part.at[k, 0], ret_ref.at[me_e], (me_e ^ k, me_t))
    back_in = lambda k: remote(11, k, part.at[k, 0], ret_ref.at[me_e ^ k], (me_e ^ k, me_t))

    place = me_e * members + me_t
    last = count * members - 1
    above = lax.rem(place + last, last + 1)
    below = lax.rem(place + 1, last + 1)
    strips = [
        pltpu.make_async_remote_copy(
            src_ref=raw_ref, dst_ref=halo.at[i], send_sem=halo_send.at[i], recv_sem=halo_recv.at[i],
            device_id=(to // members, lax.rem(to, members)), device_id_type=MESH,
        )
        for i, to in enumerate((below, above))
    ]
    greet(
        [(me_e ^ k, me_t) for k in range(1, count)]
        + [near, far, cross[3]]
        + [(to // members, lax.rem(to, members)) for to in (below, above)]
    )
    for strip_copy in strips:
        strip_copy.start()

    routes = routes_ref[...]
    hot = routes == lax.broadcasted_iota(jnp.int32, (tokens, experts), 1)
    earlier = lax.broadcasted_iota(jnp.int32, (tokens, tokens), 1) < lax.broadcasted_iota(
        jnp.int32, (tokens, tokens), 0
    )
    before = mm(earlier.astype(BF), hot.astype(BF))
    pos = jnp.sum(jnp.where(hot, before, 0.0), axis=1, keepdims=True).astype(jnp.int32)
    slot_ref[...] = routes * cap + pos

    def selector():
        return (
            slot_ref[...] == lax.broadcasted_iota(jnp.int32, (tokens, experts * cap), 1)
        ).astype(BF)

    def scatter(values, sent_ref, grp, move):
        sent_ref[...] = mm(selector(), values, TN).reshape(sent_ref.shape).astype(BF)
        for k in range(1, count):
            move[0](k).start()
        own = pltpu.make_async_copy(sent_ref.at[me_e], grp.at[0, 0], own_sem)
        own.start()
        own.wait()
        move[2](0).start()
        move[1](0).start()

    scatter(cot_ref[...], sent_c, grp_c, cots_moves)

    for strip_copy in strips:
        strip_copy.wait_recv()
    low = jnp.where(place > 0, halo[0].astype(F32), 0.0)
    high = jnp.where(place < last, halo[1].astype(F32), 0.0)
    raw = raw_ref[...].astype(F32)
    blank = jnp.zeros((8 - strip - 2, pixel_cols), F32)
    padded = jnp.concatenate(
        [
            part_rows
            for i in range(channels)
            for part_rows in (low[i, strip - 1 :], raw[i], high[i, :1], blank)
        ],
        axis=0,
    ).astype(BF)
    shape = (tokens, pixel_cols)
    token_of = lax.broadcasted_iota(jnp.int32, shape, 0)
    col_of = lax.broadcasted_iota(jnp.int32, shape, 1)
    pick = jnp.concatenate(
        [(col_of == token_of * PATCH + (dc - 1)).astype(F32) for dc in range(PATCH + 2)], axis=0
    ).astype(BF)
    picked = mm(pick, padded, NT)
    window = jnp.concatenate(
        [picked[dc * tokens : (dc + 1) * tokens] for dc in range(PATCH + 2)], axis=1
    ).astype(BF)
    loads[0].wait()
    win_all = mm(window, table_ref[...]).astype(BF)
    winall_ref[...] = win_all
    rep = mm(taps_ref[...], spread_of(stem).astype(BF), TN)
    cls = lax.broadcasted_iota(jnp.int32, rep.shape, 1) % CLASSES
    kernel = jnp.concatenate([jnp.where(cls == q, rep, 0.0) for q in range(CLASSES)], axis=0)
    preact = mm(win_all, kernel.astype(BF))
    preact_ref[...] = preact
    tanh_v = jnp.tanh(GELU_C * (preact + GELU_A * preact * preact * preact))
    patches = (0.5 * preact * (1.0 + tanh_v)).astype(BF)
    patches_ref[...] = patches
    loads[1].wait()
    embedded = mm(patches, embed_ref[...])
    embedded_ref[...] = embedded
    inv = lax.rsqrt(jnp.mean(embedded * embedded, axis=-1, keepdims=True) + EPSILON)
    inv_ref[...] = inv
    hidden = (embedded * inv * gain_ref[...]).astype(BF)
    hidden_ref[...] = hidden
    logits = mm(hidden, router_ref[...])
    score = jax.nn.sigmoid(jnp.sum(jnp.where(hot, logits, 0.0), axis=1, keepdims=True))
    score_ref[...] = score
    first = score.astype(BF).astype(F32)
    second = (score - first).astype(BF).astype(F32)
    third = score - first - second
    lane = lax.broadcasted_iota(jnp.int32, (tokens, 128), 1)
    tail = jnp.where(
        lane == 0, first, jnp.where(lane == 1, second, jnp.where(lane == 2, third, 0.0))
    )
    scatter(jnp.concatenate([hidden, tail.astype(BF)], axis=1), sent_r, grp_r, rows_moves)

    def forward(k, move):
        @pl.when(k > 0)
        def _():
            move[0](k).wait_recv()
            move[2](k).start()
            move[1](k).start()

    def forward_rows(p):
        for i in range(per):
            forward(p * per + i, rows_moves)

    def arrive(p, move):
        for i in range(per):
            k = p * per + i
            move[2](k).wait_recv()
            move[3](k).start()

    def settle(p, move):
        for i in range(per):
            k = p * per + i
            move[1](k).wait_recv()
            move[3](k).wait_recv()

    def flat(ref, p):
        blocks = ref[pl.ds(p * per, per)]
        if cap % 16:
            blocks = blocks.astype(F32)
        return blocks.reshape(batch, ref.shape[-1])

    def gather(p):
        at = pl.ds(pl.multiple_of(p * batch, batch), batch)
        rows = flat(grp_r, p)
        weight = jnp.sum(rows[:, width:].astype(F32), axis=1, keepdims=True)
        rows_all[at, :] = rows[:, :width].astype(BF)
        cots_all[at, :] = (weight * flat(grp_c, p).astype(F32)).astype(BF)

    tile = 256

    def compute(p):
        at = pl.ds(pl.multiple_of(p * batch, batch), batch)

        @pl.loop(0, share // tile)
        def _(f):
            cols = pl.ds(pl.multiple_of(f * tile, tile), tile)
            gate = mm(rows_all[at, :], wg[:, cols])
            up = mm(rows_all[at, :], wu[:, cols])
            act_cot = mm(cots_all[at, :], wd[cols, :], NT)
            sig = jax.nn.sigmoid(gate)
            activated = gate * sig
            act_all[at, cols] = (activated * up).astype(BF)
            gcot_all[at, cols] = (act_cot * up * (sig * (1.0 + gate * (1.0 - sig)))).astype(BF)
            ucot_all[at, cols] = (act_cot * activated).astype(BF)

        @pl.loop(0, width // tile)
        def _(x):
            cols = pl.ds(pl.multiple_of(x * tile, tile), tile)
            out = mm(act_all[at, :], wd[:, cols])
            back_cot = mm(gcot_all[at, :], wg[cols, :], NT) + mm(ucot_all[at, :], wu[cols, :], NT)
            both = jnp.concatenate(
                [out.reshape(per, members, cap, tile), back_cot.reshape(per, members, cap, tile)],
                axis=2,
            )
            part[pl.ds(p * per, per), :, :, cols] = both.astype(BF)

    def reduce_near(p):
        for i in range(per):
            k = p * per + i
            sum_near_a(k).wait_recv()
            sum_near_b(k).wait_recv()
            part[k, 2] = (part[k, 2].astype(F32) + rx1[k, 1].astype(F32)).astype(BF)
            sum_far(k).start()

    def reduce_far(p):
        for i in range(per):
            k = p * per + i
            sum_far(k).wait_recv()
            part[k, 0] = (
                part[k, 0].astype(F32) + rx1[k, 0].astype(F32) + rx2[k].astype(F32)
            ).astype(BF)

            @pl.when(k > 0)
            def _():
                back(k).start()

    @pl.loop(1, count)
    def _(k):
        forward(k, cots_moves)

    forward_rows(0)
    for load in loads[2:]:
        load.wait()

    @pl.loop(0, steps)
    def _(p):
        arrive(p, cots_moves)

        @pl.when(p < steps - 1)
        def _():
            forward_rows(p + 1)

        arrive(p, rows_moves)
        settle(p, cots_moves)
        settle(p, rows_moves)
        gather(p)
        compute(p)
        for i in range(per):
            k = p * per + i
            sum_near_a(k).start()
            sum_near_b(k).start()

        @pl.when(p >= 1)
        def _():
            reduce_near(p - 1)

        @pl.when(p >= 2)
        def _():
            reduce_far(p - 2)

    half = 256

    def grads(j, lhs, rhs, out_ref):
        n = width // half

        def store(c):
            return pltpu.make_async_copy(
                stage.at[j, c], out_ref.at[0, pl.ds(pl.multiple_of(c * half, half), half), :],
                store_sem.at[j, c],
            )

        @pl.loop(0, n)
        def _(c):
            at = pl.ds(pl.multiple_of(c * half, half), half)
            stage[j, c] = mm(lhs[:, at], rhs[...], TN)
            store(c).start()

        def finish():
            for c in range(n):
                store(c).wait()

        return finish

    reduce_near(steps - 1)
    if steps >= 2:
        reduce_far(steps - 2)
    ends = [grads(0, rows_all, gcot_all, ggate_ref)]
    reduce_far(steps - 1)
    own_back = pltpu.make_async_copy(part.at[0, 0], ret_ref.at[me_e], own_sem)
    own_back.start()
    ends.append(grads(1, rows_all, ucot_all, gup_ref))
    own_back.wait()
    for k in range(1, count):
        back_in(k).wait_recv()

    ret = ret_ref[...]
    if cap % 16:
        ret = ret.astype(F32)
    out_flat = ret[:, :cap].reshape(experts * cap, width).astype(BF)
    cot_flat = ret[:, cap:].reshape(experts * cap, width).astype(BF)
    select = selector()
    score = score_ref[...]
    out_wide = mm(select, out_flat)
    mix_ref[...] = (score * out_wide).astype(BF)
    score_grad = jnp.sum(cot_ref[...].astype(F32) * out_wide, axis=1, keepdims=True)
    local_grad = score_grad * score * (1.0 - score)
    hot = routes_ref[...] == lax.broadcasted_iota(jnp.int32, (tokens, experts), 1)
    logit_cot = jnp.where(hot, local_grad, 0.0).astype(BF)
    router_part = mm(logit_cot, hidden_ref[...], TN)
    upstream = mm(select, cot_flat) + mm(logit_cot, router_ref[...], NT)
    inv = inv_ref[...]
    normed = embedded_ref[...] * inv
    scaled = upstream * gain_ref[...]
    embed_cot = (
        inv * (scaled - normed * jnp.mean(scaled * normed, axis=1, keepdims=True))
    ).astype(BF)
    gain_part = jnp.sum(upstream * normed, axis=0, keepdims=True)
    patches = patches_ref[...]
    for c in range(0, chunks, 2):
        both = mm(patches, embed_cot[:, c * lanes : (c + 2) * lanes], TN).astype(BF)
        eb[c] = both[:, :lanes]
        eb[c + 1] = both[:, lanes:]

    def reduced(kind, k, src, dst, device):
        return pltpu.make_async_remote_copy(
            src_ref=src, dst_ref=dst, send_sem=red_send.at[kind, k], recv_sem=red_recv.at[kind, k],
            device_id=device, device_id_type=MESH,
        )

    sent = []

    def send(*args):
        copy = reduced(*args)
        copy.start()
        sent.append(copy)

    other = pl.ds((1 - b) * 4, 4)
    mine = pl.ds(b * 4, 4)
    send(0, 0, eb.at[other], e_rx1, near)

    preact = preact_ref[...]
    patch_cot = mm(embed_cot, embed_ref[...], NT)
    tanh_v = jnp.tanh(GELU_C * (preact + GELU_A * preact * preact * preact))
    slope = 0.5 * (1.0 + tanh_v) + 0.5 * preact * (1.0 - tanh_v * tanh_v) * GELU_C * (
        1.0 + 3.0 * GELU_A * preact * preact
    )
    preact_cot = (patch_cot * slope).astype(BF)
    cls = lax.broadcasted_iota(jnp.int32, (TAPS, patch_dim), 1) % CLASSES
    taps_all = mm(winall_ref[...], preact_cot, TN)
    taps = jnp.zeros((TAPS, patch_dim), F32)
    for q in range(CLASSES):
        taps = taps + jnp.where(cls == q, taps_all[q * TAPS : (q + 1) * TAPS], 0.0)
    stem_part = mm(spread_of(stem).astype(F32), taps, NT, lax.Precision.HIGHEST)
    stem_part = jnp.concatenate([stem_part, jnp.zeros((stem, lanes - TAPS), F32)], axis=1)
    gain_rows = jnp.broadcast_to(gain_part, (8, width))
    for c in range(chunks):
        at = slice(c * lanes, (c + 1) * lanes)
        sb[c, :experts] = router_part[:, at]
        sb[c, experts : experts + 8] = gain_rows[:, at]
        sb[c, experts + 8 :] = (
            stem_part[c * 8 : c * 8 + 8] if c * 8 < stem else jnp.zeros((8, lanes), F32)
        )
    send(1, 0, sb.at[other], s_rx1, near)

    reduced(0, 0, eb.at[other], e_rx1, near).wait_recv()
    for c in range(4):
        e_acc1[c] = (eb[b * 4 + c].astype(F32) + e_rx1[c].astype(F32)).astype(BF)
    for r in range(1, 4):
        send(2, r, e_acc1.at[g ^ r], e_rx2.at[r], cross[r])
    ends.append(grads(2, act_all, cots_all, gdown_ref))
    reduced(1, 0, sb.at[other], s_rx1, near).wait_recv()
    for c in range(4):
        s_acc1[c] = sb[b * 4 + c] + s_rx1[c]
    for r in range(1, 4):
        send(3, r, s_acc1.at[g ^ r], s_rx2.at[r], cross[r])
    for r in range(1, 4):
        reduced(2, r, e_acc1.at[g ^ r], e_rx2.at[r], cross[r]).wait_recv()
    e_acc2[...] = (
        e_acc1[g].astype(F32) + e_rx2[1].astype(F32) + e_rx2[2].astype(F32) + e_rx2[3].astype(F32)
    ).astype(BF)
    rows_of = lambda i: pl.ds(pl.multiple_of(i * piece, piece), piece)
    for r in range(1, z_count):
        send(4, r, e_acc2.at[rows_of(z ^ r)], e_rx3.at[r], along[r])
    for r in range(1, 4):
        reduced(3, r, s_acc1.at[g ^ r], s_rx2.at[r], cross[r]).wait_recv()
    s_rx3[z] = s_acc1[g] + s_rx2[1] + s_rx2[2] + s_rx2[3]
    for r in range(1, z_count):
        send(5, r, s_rx3.at[z], s_rx3.at[z], along[r])
    total = e_acc2[rows_of(z), :].astype(F32)
    for r in range(1, z_count):
        reduced(4, r, e_acc2.at[rows_of(z ^ r)], e_rx3.at[r], along[r]).wait_recv()
        total = total + e_rx3[r].astype(F32)
    e_piece[...] = total.astype(BF)
    own = b * 4 + g
    cols_of = lambda i: pl.ds(pl.multiple_of(i * lanes, lanes), lanes)
    for r in range(1, z_count):
        send(6, r, e_piece, big_ref.at[rows_of(z), cols_of(own)], along[r])
    big_ref[rows_of(z), cols_of(own)] = total.astype(BF)
    for r in range(1, z_count):
        reduced(5, r, s_rx3.at[z], s_rx3.at[z ^ r], along[r]).wait_recv()
    s_total = s_rx3[0]
    for i in range(1, z_count):
        s_total = s_total + s_rx3[i]
    small_ref[own] = s_total
    for r in range(1, 4):
        send(7, r, small_ref.at[own], small_ref.at[own], cross[r])
    for r in range(1, z_count):
        reduced(6, r, e_piece, big_ref.at[rows_of(z ^ r), cols_of(own)], along[r]).wait_recv()
    for r in range(1, 4):
        send(8, r, big_ref.at[:, cols_of(own)], big_ref.at[:, cols_of(own)], cross[r])
    for r in range(1, 4):
        reduced(7, r, small_ref.at[own], small_ref.at[b * 4 + (g ^ r)], cross[r]).wait_recv()
    send(9, 0, small_ref.at[mine], small_ref.at[mine], near)
    send(10, 0, big_ref.at[:, cols_of(own)], big_ref.at[:, cols_of(own)], near)
    for r in range(1, 4):
        theirs = b * 4 + (g ^ r)
        reduced(8, r, big_ref.at[:, cols_of(own)], big_ref.at[:, cols_of(theirs)], cross[r]).wait_recv()
        send(10, r, big_ref.at[:, cols_of(theirs)], big_ref.at[:, cols_of(theirs)], near)
    reduced(9, 0, small_ref.at[mine], small_ref.at[other], near).wait_recv()
    for r in range(4):
        theirs = (1 - b) * 4 + (g ^ r)
        reduced(10, r, big_ref.at[:, cols_of(theirs)], big_ref.at[:, cols_of(theirs)], near).wait_recv()
    for copy in sent:
        copy.wait_send()
    for copy in strips:
        copy.wait_send()

    @pl.loop(0, count)
    def _(k):
        @pl.when(k > 0)
        def _():
            rows_moves[0](k).wait_send()
            cots_moves[0](k).wait_send()
            back(k).wait_send()

        for copy in rows_moves[1:] + cots_moves[1:] + (sum_near_a, sum_near_b, sum_far):
            copy(k).wait_send()

    for end in ends:
        end()


def local(
    raw_tiles, stem_weight, embed_weight, norm_gain, router_weight, w_gate, w_up, w_down, routes,
    cotangent,
):
    tokens, width = cotangent.shape
    owners, members = lax.axis_size("de"), lax.axis_size("tp")
    experts = w_gate.shape[0] * owners
    cap = 2 * tokens // experts
    share = w_gate.shape[2]
    channels = raw_tiles.shape[0]
    stem = stem_weight.shape[0]
    patch_dim = embed_weight.shape[0]
    total = owners * members * cap
    shape = jax.ShapeDtypeStruct
    table = jnp.asarray(tap_table(channels), BF)
    taps = jnp.pad(stem_weight.reshape(stem, channels * 9), ((0, 0), (0, TAPS - channels * 9)))
    anywhere = pl.BlockSpec(memory_space=pl.ANY)
    lanes = width // 8
    z_count = owners // 2
    small_rows = experts + 16
    piece = patch_dim // z_count
    vmem, dma = pltpu.VMEM, pltpu.SemaphoreType.DMA
    mix, big, small, grad_gate, grad_up, grad_down = pl.pallas_call(
        step_kernel,
        out_shape=(
            shape((tokens, width), BF),
            shape((patch_dim, width), BF),
            shape((8, small_rows, lanes), F32),
            shape(w_gate.shape, F32),
            shape(w_up.shape, F32),
            shape(w_down.shape, F32),
        ),
        in_specs=[VMEM] * 6 + [anywhere] * 5,
        out_specs=(VMEM,) * 3 + (anywhere,) * 3,
        scratch_shapes=[
            vmem(table.shape, BF),
            vmem(embed_weight.shape, BF),
            vmem((width, share), BF),
            vmem((width, share), BF),
            vmem((share, width), BF),
            vmem((2,) + raw_tiles.shape, BF),
            vmem((experts, cap, width + 128), BF),
            vmem((experts, cap, width), BF),
            vmem((owners, members, cap, width + 128), BF),
            vmem((owners, members, cap, width), BF),
            vmem((owners, members, 2 * cap, width), BF),
            vmem((owners, 2, 2 * cap, width), BF),
            vmem((owners, 2 * cap, width), BF),
            vmem((owners, 2 * cap, width), BF),
            vmem((total, width), BF),
            vmem((total, width), BF),
            vmem((total, share), BF),
            vmem((total, share), BF),
            vmem((total, share), BF),
            vmem((3, width // 256, 256, width), F32),
            vmem((tokens, patch_dim), F32),
            vmem((tokens, patch_dim), BF),
            vmem((tokens, width), F32),
            vmem((tokens, 1), F32),
            vmem((tokens, width), BF),
            vmem((tokens, 1), F32),
            vmem((tokens, 1), jnp.int32),
            vmem((tokens, CLASSES * TAPS), BF),
            vmem((8, patch_dim, lanes), BF),
            vmem((4, patch_dim, lanes), BF),
            vmem((4, patch_dim, lanes), BF),
            vmem((4, patch_dim, lanes), BF),
            vmem((patch_dim, lanes), BF),
            vmem((z_count, piece, lanes), BF),
            vmem((piece, lanes), BF),
            vmem((8, small_rows, lanes), F32),
            vmem((4, small_rows, lanes), F32),
            vmem((4, small_rows, lanes), F32),
            vmem((4, small_rows, lanes), F32),
            vmem((z_count, small_rows, lanes), F32),
            dma((5,)),
            dma,
            dma((3, width // 256)),
            dma((2,)),
            dma((2,)),
            dma((12, owners)),
            dma((12, owners)),
            dma((11, max(4, z_count))),
            dma((11, max(4, z_count))),
        ],
        compiler_params=pltpu.CompilerParams(
            vmem_limit_bytes=58 << 20, collective_id=1, has_side_effects=True
        ),
        name="step",
    )(
        raw_tiles, taps, norm_gain.reshape(1, width), router_weight, routes, cotangent,
        table, embed_weight, w_gate, w_up, w_down,
    )
    grad_router = small[:, :experts].transpose(0, 2, 1).reshape(width, experts)
    grad_gain = small[:, experts].reshape(width)
    taps_grad = small[: stem // 8, experts + 8 :].reshape(stem, lanes)[:, : channels * 9]
    return (
        mix, grad_gate, grad_up, grad_down, grad_router, grad_gain, big.astype(F32),
        taps_grad.reshape(stem_weight.shape),
    )


def solution(mesh):
    tiles = P(("de", "tp"), None)
    columns, rows = P("de", None, "tp"), P("de", "tp", None)
    return jax.shard_map(
        local,
        mesh=mesh,
        in_specs=(
            P(None, ("de", "tp"), None), P(), P(), P(), P(), columns, columns, rows, tiles, tiles,
        ),
        out_specs=(tiles, columns, columns, rows, P(), P(), P(), P()),
        check_vma=False,
    )
```

```python
import jax
import jax.numpy as jnp
import numpy as np
from jax import lax
from jax.experimental import pallas as pl
from jax.experimental.pallas import tpu as pltpu
from jax.sharding import PartitionSpec as P

PATCH = 4
GELU_C = 0.7978845608028654
GELU_A = 0.044715
EPSILON = 1e-06
TAPS = 40
CLASSES = PATCH * PATCH
MESH = pl.DeviceIdType.MESH
BF = jnp.bfloat16
F32 = jnp.float32
VMEM = pl.BlockSpec(memory_space=pltpu.VMEM)
NT = (((1,), (1,)), ((), ()))
TN = (((0,), (0,)), ((), ()))


def mm(a, b, dims=(((1,), (0,)), ((), ())), precision=None):
    return lax.dot_general(a, b, dims, preferred_element_type=F32, precision=precision)


def tap_table(channels):
    side = PATCH + 2
    table = np.zeros((side, channels * 8, CLASSES * TAPS), np.float32)
    for q in range(CLASSES):
        for i in range(channels):
            for a in range(3):
                for b in range(3):
                    table[q % PATCH + b, i * 8 + q // PATCH + a, q * TAPS + i * 9 + a * 3 + b] = 1.0
    return table.reshape(side * channels * 8, CLASSES * TAPS)


def spread_of(stem):
    return (
        lax.broadcasted_iota(jnp.int32, (stem, stem * CLASSES), 0)
        == lax.broadcasted_iota(jnp.int32, (stem, stem * CLASSES), 1) // CLASSES
    )


def greet(devices):
    barrier = pltpu.get_barrier_semaphore()
    for device in devices:
        pl.semaphore_signal(barrier, inc=1, device_id=device, device_id_type=MESH)
    pl.semaphore_wait(barrier, len(devices))


def step_kernel(
    raw_ref, taps_ref, gain_ref, router_ref, routes_ref, cot_ref,
    table_hbm, embed_hbm, gate_ref, up_ref, down_ref,
    mix_ref, embed_out, router_out, gain_out, stem_out, ggate_ref, gup_ref, gdown_ref,
    table_ref, embed_ref, wg, wu, wd, halo, sent_r, sent_c, grp_r, grp_c, part, rx1, rx2, ret_ref,
    rows_all, cots_all, act_all, gcot_all, ucot_all, stage,
    preact_ref, patches_ref, embedded_ref, inv_ref, hidden_ref, score_ref, slot_ref, winall_ref,
    eb, e_rx1, e_acc1, e_rx2, e_acc2, e_rx3, e_piece, sb, s_rx1, s_acc1, s_rx2, s_rx3,
    big_ref, small_ref, load_sem, own_sem, store_sem, halo_send, halo_recv, send_sem, recv_sem, red_send, red_recv,
):
    count, members, cap, width = grp_c.shape
    tokens = cot_ref.shape[0]
    experts = count
    share = wg.shape[1]
    stem = taps_ref.shape[0]
    channels, strip, pixel_cols = raw_ref.shape
    me_e, me_t = lax.axis_index("de"), lax.axis_index("tp")
    batch = 256
    per = batch // (members * cap)
    steps = count // per
    chunks, patch_dim, lanes = eb.shape
    z_count = e_rx3.shape[0]
    piece = patch_dim // z_count
    b, g, z = me_t & 1, (me_t >> 1) * 2 + (me_e & 1), me_e >> 1
    near, far = (me_e, me_t ^ 1), (me_e, me_t ^ 2)
    cross = [None] + [(me_e ^ (r & 1), me_t ^ (r & 2)) for r in range(1, 4)]
    along = [None] + [(me_e ^ (2 * r), me_t) for r in range(1, z_count)]
    loads = [
        pltpu.make_async_copy(src, dst, load_sem.at[i])
        for i, (src, dst) in enumerate(
            (
                (table_hbm, table_ref), (embed_hbm, embed_ref), (gate_ref.at[0], wg),
                (up_ref.at[0], wu), (down_ref.at[0], wd),
            )
        )
    ]
    for load in loads:
        load.start()

    def partner(k):
        return me_e ^ (k // 2 + k % 2 * (count // 2))

    def remote(kind, k, src, dst, device):
        return pltpu.make_async_remote_copy(
            src_ref=src, dst_ref=dst, send_sem=send_sem.at[kind, k], recv_sem=recv_sem.at[kind, k],
            device_id=device, device_id_type=MESH,
        )

    def moves(base, sent_ref, grp):
        return (
            lambda k: remote(base, k, sent_ref.at[partner(k)], grp.at[k, 0], (partner(k), me_t)),
            lambda k: remote(base + 1, k, grp.at[k, 0], grp.at[k, 1], near),
            lambda k: remote(base + 2, k, grp.at[k, 0], grp.at[k, 2], far),
            lambda k: remote(base + 3, k, grp.at[k, 2], grp.at[k, 3], near),
        )

    rows_moves = moves(0, sent_r, grp_r)
    cots_moves = moves(4, sent_c, grp_c)
    sum_near_a = lambda k: remote(8, k, part.at[k, 1], rx1.at[k, 0], near)
    sum_near_b = lambda k: remote(9, k, part.at[k, 3], rx1.at[k, 1], near)
    sum_far = lambda k: remote(10, k, part.at[k, 2], rx2.at[k], far)
    back = lambda k: remote(11, k, part.at[k, 0], ret_ref.at[me_e], (partner(k), me_t))
    back_in = lambda k: remote(11, k, part.at[k, 0], ret_ref.at[partner(k)], (partner(k), me_t))

    place = me_e * members + me_t
    last = count * members - 1
    above = lax.rem(place + last, last + 1)
    below = lax.rem(place + 1, last + 1)
    strips = [
        pltpu.make_async_remote_copy(
            src_ref=raw_ref, dst_ref=halo.at[i], send_sem=halo_send.at[i], recv_sem=halo_recv.at[i],
            device_id=(to // members, lax.rem(to, members)), device_id_type=MESH,
        )
        for i, to in enumerate((below, above))
    ]
    greet(
        [(me_e ^ k, me_t) for k in range(1, count)]
        + [near, far, cross[3]]
        + [(to // members, lax.rem(to, members)) for to in (below, above)]
    )
    for strip_copy in strips:
        strip_copy.start()

    routes = routes_ref[...]
    hot = routes == lax.broadcasted_iota(jnp.int32, (tokens, experts), 1)
    earlier = lax.broadcasted_iota(jnp.int32, (tokens, tokens), 1) < lax.broadcasted_iota(
        jnp.int32, (tokens, tokens), 0
    )
    before = mm(earlier.astype(BF), hot.astype(BF))
    pos = jnp.sum(jnp.where(hot, before, 0.0), axis=1, keepdims=True).astype(jnp.int32)
    slot_ref[...] = routes * cap + pos

    def selector():
        return (
            slot_ref[...] == lax.broadcasted_iota(jnp.int32, (tokens, experts * cap), 1)
        ).astype(BF)

    def scatter(values, sent_ref, grp, move, window_of):
        sent_ref[...] = mm(selector(), values, TN).reshape(sent_ref.shape).astype(BF)
        for k in range(1, window_of):
            move[0](k).start()
        own = pltpu.make_async_copy(sent_ref.at[me_e], grp.at[0, 0], own_sem)
        own.start()
        own.wait()
        move[2](0).start()
        move[1](0).start()

    scatter(cot_ref[...], sent_c, grp_c, cots_moves, count)

    for strip_copy in strips:
        strip_copy.wait_recv()
    low = jnp.where(place > 0, halo[0].astype(F32), 0.0)
    high = jnp.where(place < last, halo[1].astype(F32), 0.0)
    raw = raw_ref[...].astype(F32)
    blank = jnp.zeros((8 - strip - 2, pixel_cols), F32)
    padded = jnp.concatenate(
        [
            part_rows
            for i in range(channels)
            for part_rows in (low[i, strip - 1 :], raw[i], high[i, :1], blank)
        ],
        axis=0,
    ).astype(BF)
    shape = (tokens, pixel_cols)
    token_of = lax.broadcasted_iota(jnp.int32, shape, 0)
    col_of = lax.broadcasted_iota(jnp.int32, shape, 1)
    pick = jnp.concatenate(
        [(col_of == token_of * PATCH + (dc - 1)).astype(F32) for dc in range(PATCH + 2)], axis=0
    ).astype(BF)
    picked = mm(pick, padded, NT)
    window = jnp.concatenate(
        [picked[dc * tokens : (dc + 1) * tokens] for dc in range(PATCH + 2)], axis=1
    ).astype(BF)
    loads[0].wait()
    win_all = mm(window, table_ref[...]).astype(BF)
    winall_ref[...] = win_all
    rep = mm(taps_ref[...], spread_of(stem).astype(BF), TN)
    cls = lax.broadcasted_iota(jnp.int32, rep.shape, 1) % CLASSES
    kernel = jnp.concatenate([jnp.where(cls == q, rep, 0.0) for q in range(CLASSES)], axis=0)
    preact = mm(win_all, kernel.astype(BF))
    preact_ref[...] = preact
    tanh_v = jnp.tanh(GELU_C * (preact + GELU_A * preact * preact * preact))
    patches = (0.5 * preact * (1.0 + tanh_v)).astype(BF)
    patches_ref[...] = patches
    loads[1].wait()
    embedded = mm(patches, embed_ref[...])
    embedded_ref[...] = embedded
    inv = lax.rsqrt(jnp.mean(embedded * embedded, axis=-1, keepdims=True) + EPSILON)
    inv_ref[...] = inv
    hidden = (embedded * inv * gain_ref[...]).astype(BF)
    hidden_ref[...] = hidden
    logits = mm(hidden, router_ref[...])
    score = jax.nn.sigmoid(jnp.sum(jnp.where(hot, logits, 0.0), axis=1, keepdims=True))
    score_ref[...] = score
    first = score.astype(BF).astype(F32)
    second = (score - first).astype(BF).astype(F32)
    third = score - first - second
    lane = lax.broadcasted_iota(jnp.int32, (tokens, 128), 1)
    tail = jnp.where(
        lane == 0, first, jnp.where(lane == 1, second, jnp.where(lane == 2, third, 0.0))
    )
    scatter(jnp.concatenate([hidden, tail.astype(BF)], axis=1), sent_r, grp_r, rows_moves, 2)

    def forward(k, move):
        @pl.when(k > 0)
        def _():
            move[0](k).wait_recv()
            move[2](k).start()
            move[1](k).start()

    def forward_rows(p):
        for i in range(per):
            forward(p * per + i, rows_moves)

    def arrive(p, move):
        for i in range(per):
            k = p * per + i
            move[2](k).wait_recv()
            move[3](k).start()

    def settle(p, move):
        for i in range(per):
            k = p * per + i
            move[1](k).wait_recv()
            move[3](k).wait_recv()

    def flat(ref, p):
        blocks = ref[pl.ds(p * per, per)]
        if cap % 16:
            blocks = blocks.astype(F32)
        return blocks.reshape(batch, ref.shape[-1])

    def gather(p):
        at = pl.ds(pl.multiple_of(p * batch, batch), batch)
        rows = flat(grp_r, p)
        weight = jnp.sum(rows[:, width:].astype(F32), axis=1, keepdims=True)
        rows_all[at, :] = rows[:, :width].astype(BF)
        cots_all[at, :] = (weight * flat(grp_c, p).astype(F32)).astype(BF)

    tile = 256

    def compute(p):
        at = pl.ds(pl.multiple_of(p * batch, batch), batch)

        @pl.loop(0, share // tile)
        def _(f):
            cols = pl.ds(pl.multiple_of(f * tile, tile), tile)
            gate = mm(rows_all[at, :], wg[:, cols])
            up = mm(rows_all[at, :], wu[:, cols])
            act_cot = mm(cots_all[at, :], wd[cols, :], NT)
            sig = jax.nn.sigmoid(gate)
            activated = gate * sig
            act_all[at, cols] = (activated * up).astype(BF)
            gcot_all[at, cols] = (act_cot * up * (sig * (1.0 + gate * (1.0 - sig)))).astype(BF)
            ucot_all[at, cols] = (act_cot * activated).astype(BF)

        @pl.loop(0, width // tile)
        def _(x):
            cols = pl.ds(pl.multiple_of(x * tile, tile), tile)
            out = mm(act_all[at, :], wd[:, cols])
            back_cot = mm(gcot_all[at, :], wg[cols, :], NT) + mm(ucot_all[at, :], wu[cols, :], NT)
            both = jnp.concatenate(
                [out.reshape(per, members, cap, tile), back_cot.reshape(per, members, cap, tile)],
                axis=2,
            )
            part[pl.ds(p * per, per), :, :, cols] = both.astype(BF)

    def reduce_near(p):
        for i in range(per):
            k = p * per + i
            sum_near_a(k).wait_recv()
            sum_near_b(k).wait_recv()
            part[k, 2] = (part[k, 2].astype(F32) + rx1[k, 1].astype(F32)).astype(BF)
            sum_far(k).start()

    def reduce_far(p):
        for i in range(per):
            k = p * per + i
            sum_far(k).wait_recv()
            part[k, 0] = (
                part[k, 0].astype(F32) + rx1[k, 0].astype(F32) + rx2[k].astype(F32)
            ).astype(BF)

            @pl.when(k > 0)
            def _():
                back(k).start()

    @pl.loop(1, count)
    def _(k):
        forward(k, cots_moves)

        @pl.when(k < count - 1)
        def _():
            rows_moves[0](k + 1).start()

    forward_rows(0)
    for load in loads[2:]:
        load.wait()

    @pl.loop(0, steps)
    def _(p):
        arrive(p, cots_moves)

        @pl.when(p < steps - 1)
        def _():
            forward_rows(p + 1)

        arrive(p, rows_moves)
        settle(p, cots_moves)
        settle(p, rows_moves)
        gather(p)

        @pl.when(p >= 1)
        def _():
            reduce_near(p - 1)

        compute(p)
        for i in range(per):
            k = p * per + i
            sum_near_a(k).start()
            sum_near_b(k).start()

        @pl.when(p >= 1)
        def _():
            reduce_far(p - 1)

    half = 256

    def grads(j, lhs, rhs, out_ref):
        n = width // half

        def store(c):
            return pltpu.make_async_copy(
                stage.at[j, c % 2], out_ref.at[0, pl.ds(pl.multiple_of(c * half, half), half), :],
                store_sem.at[j, c % 2],
            )

        @pl.loop(0, n)
        def _(c):
            @pl.when(c >= 2)
            def _():
                store(c - 2).wait()

            at = pl.ds(pl.multiple_of(c * half, half), half)
            stage[j, c % 2] = mm(lhs[:, at], rhs[...], TN)
            store(c).start()

        def finish():
            for c in range(max(0, n - 2), n):
                store(c).wait()

        return finish

    reduce_near(steps - 1)
    ends = [grads(0, rows_all, gcot_all, ggate_ref)]
    reduce_far(steps - 1)
    own_back = pltpu.make_async_copy(part.at[0, 0], ret_ref.at[me_e], own_sem)
    own_back.start()
    ends.append(grads(1, rows_all, ucot_all, gup_ref))
    own_back.wait()
    for k in range(1, count):
        back_in(k).wait_recv()

    ret = ret_ref[...]
    if cap % 16:
        ret = ret.astype(F32)
    out_flat = ret[:, :cap].reshape(experts * cap, width).astype(BF)
    cot_flat = ret[:, cap:].reshape(experts * cap, width).astype(BF)
    select = selector()
    score = score_ref[...]
    out_wide = mm(select, out_flat)
    mix_ref[...] = (score * out_wide).astype(BF)
    score_grad = jnp.sum(cot_ref[...].astype(F32) * out_wide, axis=1, keepdims=True)
    local_grad = score_grad * score * (1.0 - score)
    hot = routes_ref[...] == lax.broadcasted_iota(jnp.int32, (tokens, experts), 1)
    logit_cot = jnp.where(hot, local_grad, 0.0).astype(BF)
    router_part = mm(logit_cot, hidden_ref[...], TN)
    upstream = mm(select, cot_flat) + mm(logit_cot, router_ref[...], NT)
    inv = inv_ref[...]
    normed = embedded_ref[...] * inv
    scaled = upstream * gain_ref[...]
    embed_cot = (
        inv * (scaled - normed * jnp.mean(scaled * normed, axis=1, keepdims=True))
    ).astype(BF)
    gain_part = jnp.sum(upstream * normed, axis=0, keepdims=True)
    patches = patches_ref[...]
    for c in range(0, chunks, 2):
        both = mm(patches, embed_cot[:, c * lanes : (c + 2) * lanes], TN).astype(BF)
        eb[c] = both[:, :lanes]
        eb[c + 1] = both[:, lanes:]

    def reduced(kind, k, src, dst, device):
        return pltpu.make_async_remote_copy(
            src_ref=src, dst_ref=dst, send_sem=red_send.at[kind, k], recv_sem=red_recv.at[kind, k],
            device_id=device, device_id_type=MESH,
        )

    sent = []

    def send(*args):
        copy = reduced(*args)
        copy.start()
        sent.append(copy)

    other = pl.ds((1 - b) * 4, 4)
    mine = pl.ds(b * 4, 4)
    send(0, 0, eb.at[other], e_rx1, near)

    preact = preact_ref[...]
    patch_cot = mm(embed_cot, embed_ref[...], NT)
    tanh_v = jnp.tanh(GELU_C * (preact + GELU_A * preact * preact * preact))
    slope = 0.5 * (1.0 + tanh_v) + 0.5 * preact * (1.0 - tanh_v * tanh_v) * GELU_C * (
        1.0 + 3.0 * GELU_A * preact * preact
    )
    preact_cot = (patch_cot * slope).astype(BF)
    cls = lax.broadcasted_iota(jnp.int32, (TAPS, patch_dim), 1) % CLASSES
    taps_all = mm(winall_ref[...], preact_cot, TN)
    taps = jnp.zeros((TAPS, patch_dim), F32)
    for q in range(CLASSES):
        taps = taps + jnp.where(cls == q, taps_all[q * TAPS : (q + 1) * TAPS], 0.0)
    stem_part = mm(spread_of(stem).astype(F32), taps, NT, lax.Precision.HIGHEST)
    stem_part = jnp.concatenate([stem_part, jnp.zeros((stem, lanes - TAPS), F32)], axis=1)
    gain_rows = jnp.broadcast_to(gain_part, (8, width))
    for c in range(chunks):
        at = slice(c * lanes, (c + 1) * lanes)
        sb[c, :experts] = router_part[:, at]
        sb[c, experts : experts + 8] = gain_rows[:, at]
        sb[c, experts + 8 :] = (
            stem_part[c * 8 : c * 8 + 8] if c * 8 < stem else jnp.zeros((8, lanes), F32)
        )
    send(1, 0, sb.at[other], s_rx1, near)

    reduced(0, 0, eb.at[other], e_rx1, near).wait_recv()
    for c in range(4):
        e_acc1[c] = (eb[b * 4 + c].astype(F32) + e_rx1[c].astype(F32)).astype(BF)
    for r in range(1, 4):
        send(2, r, e_acc1.at[g ^ r], e_rx2.at[r], cross[r])
    ends.append(grads(2, act_all, cots_all, gdown_ref))
    reduced(1, 0, sb.at[other], s_rx1, near).wait_recv()
    for c in range(4):
        s_acc1[c] = sb[b * 4 + c] + s_rx1[c]
    for r in range(1, 4):
        send(3, r, s_acc1.at[g ^ r], s_rx2.at[r], cross[r])
    for r in range(1, 4):
        reduced(2, r, e_acc1.at[g ^ r], e_rx2.at[r], cross[r]).wait_recv()
    e_acc2[...] = (
        e_acc1[g].astype(F32) + e_rx2[1].astype(F32) + e_rx2[2].astype(F32) + e_rx2[3].astype(F32)
    ).astype(BF)
    rows_of = lambda i: pl.ds(pl.multiple_of(i * piece, piece), piece)
    for r in range(1, z_count):
        send(4, r, e_acc2.at[rows_of(z ^ r)], e_rx3.at[r], along[r])
    for r in range(1, 4):
        reduced(3, r, s_acc1.at[g ^ r], s_rx2.at[r], cross[r]).wait_recv()
    s_rx3[z] = s_acc1[g] + s_rx2[1] + s_rx2[2] + s_rx2[3]
    for r in range(1, z_count):
        send(5, r, s_rx3.at[z], s_rx3.at[z], along[r])
    total = e_acc2[rows_of(z), :].astype(F32)
    for r in range(1, z_count):
        reduced(4, r, e_acc2.at[rows_of(z ^ r)], e_rx3.at[r], along[r]).wait_recv()
        total = total + e_rx3[r].astype(F32)
    e_piece[...] = total.astype(BF)
    own = b * 4 + g
    cols_of = lambda i: pl.ds(pl.multiple_of(i * lanes, lanes), lanes)
    for r in range(1, z_count):
        send(6, r, e_piece, big_ref.at[rows_of(z), cols_of(own)], along[r])
    big_ref[rows_of(z), cols_of(own)] = total.astype(BF)
    for r in range(1, z_count):
        reduced(5, r, s_rx3.at[z], s_rx3.at[z ^ r], along[r]).wait_recv()
    s_total = s_rx3[0]
    for i in range(1, z_count):
        s_total = s_total + s_rx3[i]
    small_ref[own] = s_total
    for r in range(1, 4):
        send(7, r, small_ref.at[own], small_ref.at[own], cross[r])
    for r in range(1, z_count):
        reduced(6, r, e_piece, big_ref.at[rows_of(z ^ r), cols_of(own)], along[r]).wait_recv()
    for r in range(1, 4):
        send(8, r, big_ref.at[:, cols_of(own)], big_ref.at[:, cols_of(own)], cross[r])
    for r in range(1, 4):
        reduced(7, r, small_ref.at[own], small_ref.at[b * 4 + (g ^ r)], cross[r]).wait_recv()
    send(9, 0, small_ref.at[mine], small_ref.at[mine], near)
    send(10, 0, big_ref.at[:, cols_of(own)], big_ref.at[:, cols_of(own)], near)
    for r in range(1, 4):
        theirs = b * 4 + (g ^ r)
        reduced(8, r, big_ref.at[:, cols_of(own)], big_ref.at[:, cols_of(theirs)], cross[r]).wait_recv()
        send(10, r, big_ref.at[:, cols_of(theirs)], big_ref.at[:, cols_of(theirs)], near)

    def widen(i):
        embed_out[:, cols_of(i)] = big_ref[:, cols_of(i)].astype(F32)

    for r in range(4):
        widen(b * 4 + (g ^ r))
    reduced(9, 0, small_ref.at[mine], small_ref.at[other], near).wait_recv()
    for r in range(4):
        theirs = (1 - b) * 4 + (g ^ r)
        reduced(10, r, big_ref.at[:, cols_of(theirs)], big_ref.at[:, cols_of(theirs)], near).wait_recv()
        widen(theirs)
    for c in range(chunks):
        at = slice(c * lanes, (c + 1) * lanes)
        router_out[:, at] = small_ref[c, :experts]
        gain_out[:, at] = small_ref[c, experts : experts + 1]
        if c * 8 < stem:
            stem_out[c * 8 : c * 8 + 8] = small_ref[c, experts + 8 :]
    for copy in sent:
        copy.wait_send()
    for copy in strips:
        copy.wait_send()

    @pl.loop(0, count)
    def _(k):
        @pl.when(k > 0)
        def _():
            rows_moves[0](k).wait_send()
            cots_moves[0](k).wait_send()
            back(k).wait_send()

        for copy in rows_moves[1:] + cots_moves[1:] + (sum_near_a, sum_near_b, sum_far):
            copy(k).wait_send()

    for end in ends:
        end()


def local(
    raw_tiles, stem_weight, embed_weight, norm_gain, router_weight, w_gate, w_up, w_down, routes,
    cotangent,
):
    tokens, width = cotangent.shape
    owners, members = lax.axis_size("de"), lax.axis_size("tp")
    experts = w_gate.shape[0] * owners
    cap = 2 * tokens // experts
    share = w_gate.shape[2]
    channels = raw_tiles.shape[0]
    stem = stem_weight.shape[0]
    patch_dim = embed_weight.shape[0]
    total = owners * members * cap
    shape = jax.ShapeDtypeStruct
    table = jnp.asarray(tap_table(channels), BF)
    taps = jnp.pad(stem_weight.reshape(stem, channels * 9), ((0, 0), (0, TAPS - channels * 9)))
    anywhere = pl.BlockSpec(memory_space=pl.ANY)
    lanes = width // 8
    z_count = owners // 2
    small_rows = experts + 16
    piece = patch_dim // z_count
    vmem, dma = pltpu.VMEM, pltpu.SemaphoreType.DMA
    mix, grad_embed, router_rows, grad_gain, taps_grad, grad_gate, grad_up, grad_down = pl.pallas_call(
        step_kernel,
        out_shape=(
            shape((tokens, width), BF),
            shape((patch_dim, width), F32),
            shape((experts, width), F32),
            shape((1, width), F32),
            shape((stem, lanes), F32),
            shape(w_gate.shape, F32),
            shape(w_up.shape, F32),
            shape(w_down.shape, F32),
        ),
        in_specs=[VMEM] * 6 + [anywhere] * 5,
        out_specs=(VMEM,) * 5 + (anywhere,) * 3,
        scratch_shapes=[
            vmem(table.shape, BF),
            vmem(embed_weight.shape, BF),
            vmem((width, share), BF),
            vmem((width, share), BF),
            vmem((share, width), BF),
            vmem((2,) + raw_tiles.shape, BF),
            vmem((experts, cap, width + 128), BF),
            vmem((experts, cap, width), BF),
            vmem((owners, members, cap, width + 128), BF),
            vmem((owners, members, cap, width), BF),
            vmem((owners, members, 2 * cap, width), BF),
            vmem((owners, 2, 2 * cap, width), BF),
            vmem((owners, 2 * cap, width), BF),
            vmem((owners, 2 * cap, width), BF),
            vmem((total, width), BF),
            vmem((total, width), BF),
            vmem((total, share), BF),
            vmem((total, share), BF),
            vmem((total, share), BF),
            vmem((3, 2, 256, width), F32),
            vmem((tokens, patch_dim), F32),
            vmem((tokens, patch_dim), BF),
            vmem((tokens, width), F32),
            vmem((tokens, 1), F32),
            vmem((tokens, width), BF),
            vmem((tokens, 1), F32),
            vmem((tokens, 1), jnp.int32),
            vmem((tokens, CLASSES * TAPS), BF),
            vmem((8, patch_dim, lanes), BF),
            vmem((4, patch_dim, lanes), BF),
            vmem((4, patch_dim, lanes), BF),
            vmem((4, patch_dim, lanes), BF),
            vmem((patch_dim, lanes), BF),
            vmem((z_count, piece, lanes), BF),
            vmem((piece, lanes), BF),
            vmem((8, small_rows, lanes), F32),
            vmem((4, small_rows, lanes), F32),
            vmem((4, small_rows, lanes), F32),
            vmem((4, small_rows, lanes), F32),
            vmem((z_count, small_rows, lanes), F32),
            vmem((patch_dim, width), BF),
            vmem((8, small_rows, lanes), F32),
            dma((5,)),
            dma,
            dma((3, 2)),
            dma((2,)),
            dma((2,)),
            dma((12, owners)),
            dma((12, owners)),
            dma((11, max(4, z_count))),
            dma((11, max(4, z_count))),
        ],
        compiler_params=pltpu.CompilerParams(
            vmem_limit_bytes=52 << 20, collective_id=1, has_side_effects=True
        ),
        name="step",
    )(
        raw_tiles, taps, norm_gain.reshape(1, width), router_weight, routes, cotangent,
        table, embed_weight, w_gate, w_up, w_down,
    )
    return (
        mix, grad_gate, grad_up, grad_down, router_rows.T, grad_gain.reshape(width), grad_embed,
        taps_grad[:, : channels * 9].reshape(stem_weight.shape),
    )


def solution(mesh):
    tiles = P(("de", "tp"), None)
    columns, rows = P("de", None, "tp"), P("de", "tp", None)
    return jax.shard_map(
        local,
        mesh=mesh,
        in_specs=(
            P(None, ("de", "tp"), None), P(), P(), P(), P(), columns, columns, rows, tiles, tiles,
        ),
        out_specs=(tiles, columns, columns, rows, P(), P(), P(), P()),
        check_vma=False,
    )
```

```python
import jax
import jax.numpy as jnp
import numpy as np
from jax import lax
from jax.experimental import pallas as pl
from jax.experimental.pallas import tpu as pltpu
from jax.sharding import PartitionSpec as P

PATCH = 4
GELU_C = 0.7978845608028654
GELU_A = 0.044715
EPSILON = 1e-06
TAPS = 40
BATCH = 512
CLASSES = PATCH * PATCH
MESH = pl.DeviceIdType.MESH
BF = jnp.bfloat16
F32 = jnp.float32
VMEM = pl.BlockSpec(memory_space=pltpu.VMEM)
NT = (((1,), (1,)), ((), ()))
TN = (((0,), (0,)), ((), ()))


def mm(a, b, dims=(((1,), (0,)), ((), ())), precision=None):
    return lax.dot_general(a, b, dims, preferred_element_type=F32, precision=precision)


def tap_table(channels):
    side = PATCH + 2
    table = np.zeros((side, channels * 8, CLASSES * TAPS), np.float32)
    for q in range(CLASSES):
        for i in range(channels):
            for a in range(3):
                for b in range(3):
                    table[q % PATCH + b, i * 8 + q // PATCH + a, q * TAPS + i * 9 + a * 3 + b] = 1.0
    return table.reshape(side * channels * 8, CLASSES * TAPS)


def spread_of(stem):
    return (
        lax.broadcasted_iota(jnp.int32, (stem, stem * CLASSES), 0)
        == lax.broadcasted_iota(jnp.int32, (stem, stem * CLASSES), 1) // CLASSES
    )


def greet(devices):
    barrier = pltpu.get_barrier_semaphore()
    for device in devices:
        pl.semaphore_signal(barrier, inc=1, device_id=device, device_id_type=MESH)
    pl.semaphore_wait(barrier, len(devices))


def step_kernel(
    raw_ref, taps_ref, gain_ref, router_ref, routes_ref, cot_ref,
    table_hbm, embed_hbm, gate_ref, up_ref, down_ref,
    mix_ref, embed_out, router_out, gain_out, stem_out, ggate_ref, gup_ref, gdown_ref,
    table_ref, embed_ref, wg, wu, wd, wg_t, wu_t, wd_t, halo, sent_r, sent_c, grp_r, grp_c, part, rx1, rx2, ret_ref,
    rows_all, cots_all, act_all, gcot_all, ucot_all, stage,
    preact_ref, patches_ref, embedded_ref, inv_ref, hidden_ref, score_ref, slot_ref, winall_ref,
    eb, e_rx1, e_acc1, e_rx2, e_acc2, e_rx3, e_piece, sb, s_rx1, s_acc1, s_rx2, s_rx3,
    big_ref, small_ref, load_sem, own_sem, store_sem, halo_send, halo_recv, send_sem, recv_sem, red_send, red_recv,
):
    count, members, cap, width = grp_c.shape
    tokens = cot_ref.shape[0]
    experts = count
    share = wg.shape[1]
    stem = taps_ref.shape[0]
    channels, strip, pixel_cols = raw_ref.shape
    me_e, me_t = lax.axis_index("de"), lax.axis_index("tp")
    batch = BATCH
    per = batch // (members * cap)
    steps = count // per
    chunks, patch_dim, lanes = eb.shape
    z_count = e_rx3.shape[0]
    piece = patch_dim // z_count
    b, g, z = me_t & 1, (me_t >> 1) * 2 + (me_e & 1), me_e >> 1
    near, far = (me_e, me_t ^ 1), (me_e, me_t ^ 2)
    cross = [None] + [(me_e ^ (r & 1), me_t ^ (r & 2)) for r in range(1, 4)]
    along = [None] + [(me_e ^ (2 * r), me_t) for r in range(1, z_count)]
    loads = [
        pltpu.make_async_copy(src, dst, load_sem.at[i])
        for i, (src, dst) in enumerate(
            (
                (table_hbm, table_ref), (embed_hbm, embed_ref), (gate_ref.at[0], wg),
                (up_ref.at[0], wu), (down_ref.at[0], wd),
            )
        )
    ]
    for load in loads:
        load.start()

    def partner(k):
        return me_e ^ (k // 2 + k % 2 * (count // 2))

    def remote(kind, k, src, dst, device):
        return pltpu.make_async_remote_copy(
            src_ref=src, dst_ref=dst, send_sem=send_sem.at[kind, k], recv_sem=recv_sem.at[kind, k],
            device_id=device, device_id_type=MESH,
        )

    def moves(base, sent_ref, grp):
        return (
            lambda k: remote(base, k, sent_ref.at[partner(k)], grp.at[k, 0], (partner(k), me_t)),
            lambda k: remote(base + 1, k, grp.at[k, 0], grp.at[k, 1], near),
            lambda k: remote(base + 2, k, grp.at[k, 0], grp.at[k, 2], far),
            lambda k: remote(base + 3, k, grp.at[k, 2], grp.at[k, 3], near),
        )

    rows_moves = moves(0, sent_r, grp_r)
    cots_moves = moves(4, sent_c, grp_c)
    sum_near_a = lambda k: remote(8, k, part.at[k, 1], rx1.at[k, 0], near)
    sum_near_b = lambda k: remote(9, k, part.at[k, 3], rx1.at[k, 1], near)
    sum_far = lambda k: remote(10, k, part.at[k, 2], rx2.at[k], far)
    back = lambda k: remote(11, k, part.at[k, 0], ret_ref.at[me_e], (partner(k), me_t))
    back_in = lambda k: remote(11, k, part.at[k, 0], ret_ref.at[partner(k)], (partner(k), me_t))

    place = me_e * members + me_t
    last = count * members - 1
    above = lax.rem(place + last, last + 1)
    below = lax.rem(place + 1, last + 1)
    strips = [
        pltpu.make_async_remote_copy(
            src_ref=raw_ref, dst_ref=halo.at[i], send_sem=halo_send.at[i], recv_sem=halo_recv.at[i],
            device_id=(to // members, lax.rem(to, members)), device_id_type=MESH,
        )
        for i, to in enumerate((below, above))
    ]
    greet(
        [(me_e ^ k, me_t) for k in range(1, count)]
        + [near, far, cross[3]]
        + [(to // members, lax.rem(to, members)) for to in (below, above)]
    )
    for strip_copy in strips:
        strip_copy.start()

    routes = routes_ref[...]
    hot = routes == lax.broadcasted_iota(jnp.int32, (tokens, experts), 1)
    earlier = lax.broadcasted_iota(jnp.int32, (tokens, tokens), 1) < lax.broadcasted_iota(
        jnp.int32, (tokens, tokens), 0
    )
    before = mm(earlier.astype(BF), hot.astype(BF))
    pos = jnp.sum(jnp.where(hot, before, 0.0), axis=1, keepdims=True).astype(jnp.int32)
    slot_ref[...] = routes * cap + pos

    def selector():
        return (
            slot_ref[...] == lax.broadcasted_iota(jnp.int32, (tokens, experts * cap), 1)
        ).astype(BF)

    def scatter(values, sent_ref, grp, move, window_of):
        sent_ref[...] = mm(selector(), values, TN).reshape(sent_ref.shape).astype(BF)
        for k in range(1, window_of):
            move[0](k).start()
        own = pltpu.make_async_copy(sent_ref.at[me_e], grp.at[0, 0], own_sem)
        own.start()
        own.wait()
        move[2](0).start()
        move[1](0).start()

    scatter(cot_ref[...], sent_c, grp_c, cots_moves, count)

    for strip_copy in strips:
        strip_copy.wait_recv()
    low = jnp.where(place > 0, halo[0].astype(F32), 0.0)
    high = jnp.where(place < last, halo[1].astype(F32), 0.0)
    raw = raw_ref[...].astype(F32)
    blank = jnp.zeros((8 - strip - 2, pixel_cols), F32)
    padded = jnp.concatenate(
        [
            part_rows
            for i in range(channels)
            for part_rows in (low[i, strip - 1 :], raw[i], high[i, :1], blank)
        ],
        axis=0,
    ).astype(BF)
    shape = (tokens, pixel_cols)
    token_of = lax.broadcasted_iota(jnp.int32, shape, 0)
    col_of = lax.broadcasted_iota(jnp.int32, shape, 1)
    pick = jnp.concatenate(
        [(col_of == token_of * PATCH + (dc - 1)).astype(F32) for dc in range(PATCH + 2)], axis=0
    ).astype(BF)
    picked = mm(pick, padded, NT)
    window = jnp.concatenate(
        [picked[dc * tokens : (dc + 1) * tokens] for dc in range(PATCH + 2)], axis=1
    ).astype(BF)
    loads[0].wait()
    win_all = mm(window, table_ref[...]).astype(BF)
    winall_ref[...] = win_all
    rep = mm(taps_ref[...], spread_of(stem).astype(BF), TN)
    cls = lax.broadcasted_iota(jnp.int32, rep.shape, 1) % CLASSES
    kernel = jnp.concatenate([jnp.where(cls == q, rep, 0.0) for q in range(CLASSES)], axis=0)
    preact = mm(win_all, kernel.astype(BF))
    preact_ref[...] = preact
    tanh_v = jnp.tanh(GELU_C * (preact + GELU_A * preact * preact * preact))
    patches = (0.5 * preact * (1.0 + tanh_v)).astype(BF)
    patches_ref[...] = patches
    loads[1].wait()
    embedded = mm(patches, embed_ref[...])
    embedded_ref[...] = embedded
    inv = lax.rsqrt(jnp.mean(embedded * embedded, axis=-1, keepdims=True) + EPSILON)
    inv_ref[...] = inv
    hidden = (embedded * inv * gain_ref[...]).astype(BF)
    hidden_ref[...] = hidden
    logits = mm(hidden, router_ref[...])
    score = jax.nn.sigmoid(jnp.sum(jnp.where(hot, logits, 0.0), axis=1, keepdims=True))
    score_ref[...] = score
    first = score.astype(BF).astype(F32)
    second = (score - first).astype(BF).astype(F32)
    third = score - first - second
    lane = lax.broadcasted_iota(jnp.int32, (tokens, 128), 1)
    tail = jnp.where(
        lane == 0, first, jnp.where(lane == 1, second, jnp.where(lane == 2, third, 0.0))
    )
    scatter(jnp.concatenate([hidden, tail.astype(BF)], axis=1), sent_r, grp_r, rows_moves, 2)

    def forward(k, move):
        @pl.when(k > 0)
        def _():
            move[0](k).wait_recv()
            move[2](k).start()
            move[1](k).start()

    def forward_rows(p):
        for i in range(per):
            forward(p * per + i, rows_moves)

    def arrive(p, move):
        for i in range(per):
            k = p * per + i
            move[2](k).wait_recv()
            move[3](k).start()

    def settle(p, move):
        for i in range(per):
            k = p * per + i
            move[1](k).wait_recv()
            move[3](k).wait_recv()

    def flat(ref, p):
        blocks = ref[pl.ds(p * per, per)]
        if cap % 16:
            blocks = blocks.astype(F32)
        return blocks.reshape(batch, ref.shape[-1])

    def gather(p):
        at = pl.ds(pl.multiple_of(p * batch, batch), batch)
        rows = flat(grp_r, p)
        weight = jnp.sum(rows[:, width:].astype(F32), axis=1, keepdims=True)
        rows_all[at, :] = rows[:, :width].astype(BF)
        cots_all[at, :] = (weight * flat(grp_c, p).astype(F32)).astype(BF)

    tile = 256

    def hidden_units(p):
        at = pl.ds(pl.multiple_of(p * batch, batch), batch)

        @pl.loop(0, share // tile)
        def _(f):
            cols = pl.ds(pl.multiple_of(f * tile, tile), tile)
            gate = mm(rows_all[at, :], wg[:, cols])
            up = mm(rows_all[at, :], wu[:, cols])
            act_cot = mm(cots_all[at, :], wd_t[:, cols])
            sig = jax.nn.sigmoid(gate)
            activated = gate * sig
            act_all[at, cols] = (activated * up).astype(BF)
            gcot_all[at, cols] = (act_cot * up * (sig * (1.0 + gate * (1.0 - sig)))).astype(BF)
            ucot_all[at, cols] = (act_cot * activated).astype(BF)

    def results(p):
        at = pl.ds(pl.multiple_of(p * batch, batch), batch)

        @pl.loop(0, width // tile)
        def _(x):
            cols = pl.ds(pl.multiple_of(x * tile, tile), tile)
            out = mm(act_all[at, :], wd[:, cols])
            back_cot = mm(gcot_all[at, :], wg_t[:, cols]) + mm(ucot_all[at, :], wu_t[:, cols])
            both = jnp.concatenate(
                [out.reshape(per, members, cap, tile), back_cot.reshape(per, members, cap, tile)],
                axis=2,
            )
            part[pl.ds(p * per, per), :, :, cols] = both.astype(BF)

    def reduce_near(p):
        for i in range(per):
            k = p * per + i
            sum_near_a(k).wait_recv()
            sum_near_b(k).wait_recv()
            part[k, 2] = (part[k, 2].astype(F32) + rx1[k, 1].astype(F32)).astype(BF)
            sum_far(k).start()

    def reduce_far(p):
        for i in range(per):
            k = p * per + i
            sum_far(k).wait_recv()
            part[k, 0] = (
                part[k, 0].astype(F32) + rx1[k, 0].astype(F32) + rx2[k].astype(F32)
            ).astype(BF)

            @pl.when(k > 0)
            def _():
                back(k).start()

    for load in loads[2:]:
        load.wait()
    pieces = width // 128

    def turn(i):
        at = pl.ds(pl.multiple_of(i * 128, 128), 128)
        for plain, turned in ((wg, wg_t), (wu, wu_t), (wd, wd_t)):
            turned[:, at] = plain[at, :].T

    @pl.loop(1, count)
    def _(k):
        forward(k, cots_moves)

        @pl.when(k < count - 1)
        def _():
            rows_moves[0](k + 1).start()

        @pl.when(k <= pieces)
        def _():
            turn(k - 1)

    for i in range(count - 1, pieces):
        turn(i)
    forward_rows(0)

    @pl.loop(0, steps)
    def _(p):
        arrive(p, cots_moves)

        arrive(p, rows_moves)
        settle(p, cots_moves)
        settle(p, rows_moves)
        gather(p)

        @pl.when(p >= 1)
        def _():
            reduce_near(p - 1)

        hidden_units(p)

        @pl.when(p < steps - 1)
        def _():
            forward_rows(p + 1)

        @pl.when(p >= 1)
        def _():
            reduce_far(p - 1)

        results(p)
        for i in range(per):
            k = p * per + i
            sum_near_a(k).start()
            sum_near_b(k).start()

    half = 512

    def grads(c, lhs, pairs):
        turned = wd_t.at[pl.ds(0, half)]
        turned[...] = lhs[:, c * half : (c + 1) * half].T
        for j, rhs, out_ref in pairs:
            for n in range(width // half):
                at = pl.ds(n * half, half)

                def store(row):
                    return pltpu.make_async_copy(
                        stage.at[j, n], out_ref.at[0, pl.ds(row * half, half), at], store_sem.at[j, n]
                    )

                if c:
                    store(c - 1).wait()
                stage[j, n] = mm(turned[...], rhs[:, at])
                store(c).start()
                if c == width // half - 1:
                    ends.append(store(c))

    ends = []
    by_rows = [(0, gcot_all, ggate_ref), (1, ucot_all, gup_ref)]
    by_act = [(2, cots_all, gdown_ref)]
    reduce_near(steps - 1)
    grads(0, rows_all, by_rows)
    reduce_far(steps - 1)
    own_back = pltpu.make_async_copy(part.at[0, 0], ret_ref.at[me_e], own_sem)
    own_back.start()
    grads(1, rows_all, by_rows)
    own_back.wait()
    for k in range(1, count):
        back_in(k).wait_recv()

    ret = ret_ref[...]
    if cap % 16:
        ret = ret.astype(F32)
    out_flat = ret[:, :cap].reshape(experts * cap, width).astype(BF)
    cot_flat = ret[:, cap:].reshape(experts * cap, width).astype(BF)
    select = selector()
    score = score_ref[...]
    out_wide = mm(select, out_flat)
    mix_ref[...] = (score * out_wide).astype(BF)
    score_grad = jnp.sum(cot_ref[...].astype(F32) * out_wide, axis=1, keepdims=True)
    local_grad = score_grad * score * (1.0 - score)
    hot = routes_ref[...] == lax.broadcasted_iota(jnp.int32, (tokens, experts), 1)
    logit_cot = jnp.where(hot, local_grad, 0.0).astype(BF)
    router_part = mm(logit_cot, hidden_ref[...], TN)
    upstream = mm(select, cot_flat) + mm(logit_cot, router_ref[...], NT)
    inv = inv_ref[...]
    normed = embedded_ref[...] * inv
    scaled = upstream * gain_ref[...]
    embed_cot = (
        inv * (scaled - normed * jnp.mean(scaled * normed, axis=1, keepdims=True))
    ).astype(BF)
    gain_part = jnp.sum(upstream * normed, axis=0, keepdims=True)
    patches = patches_ref[...]
    for c in range(0, chunks, 2):
        both = mm(patches, embed_cot[:, c * lanes : (c + 2) * lanes], TN).astype(BF)
        eb[c] = both[:, :lanes]
        eb[c + 1] = both[:, lanes:]

    def reduced(kind, k, src, dst, device):
        return pltpu.make_async_remote_copy(
            src_ref=src, dst_ref=dst, send_sem=red_send.at[kind, k], recv_sem=red_recv.at[kind, k],
            device_id=device, device_id_type=MESH,
        )

    sent = []

    def send(*args):
        copy = reduced(*args)
        copy.start()
        sent.append(copy)

    other = pl.ds((1 - b) * 4, 4)
    mine = pl.ds(b * 4, 4)
    send(0, 0, eb.at[other], e_rx1, near)

    preact = preact_ref[...]
    patch_cot = mm(embed_cot, embed_ref[...], NT)
    tanh_v = jnp.tanh(GELU_C * (preact + GELU_A * preact * preact * preact))
    slope = 0.5 * (1.0 + tanh_v) + 0.5 * preact * (1.0 - tanh_v * tanh_v) * GELU_C * (
        1.0 + 3.0 * GELU_A * preact * preact
    )
    preact_cot = (patch_cot * slope).astype(BF)
    cls = lax.broadcasted_iota(jnp.int32, (TAPS, patch_dim), 1) % CLASSES
    taps_all = mm(winall_ref[...], preact_cot, TN)
    taps = jnp.zeros((TAPS, patch_dim), F32)
    for q in range(CLASSES):
        taps = taps + jnp.where(cls == q, taps_all[q * TAPS : (q + 1) * TAPS], 0.0)
    stem_part = mm(spread_of(stem).astype(F32), taps, NT, lax.Precision.HIGHEST)
    stem_part = jnp.concatenate([stem_part, jnp.zeros((stem, lanes - TAPS), F32)], axis=1)
    gain_rows = jnp.broadcast_to(gain_part, (8, width))
    for c in range(chunks):
        at = slice(c * lanes, (c + 1) * lanes)
        sb[c, :experts] = router_part[:, at]
        sb[c, experts : experts + 8] = gain_rows[:, at]
        sb[c, experts + 8 :] = (
            stem_part[c * 8 : c * 8 + 8] if c * 8 < stem else jnp.zeros((8, lanes), F32)
        )
    send(1, 0, sb.at[other], s_rx1, near)

    grads(0, act_all, by_act)
    reduced(0, 0, eb.at[other], e_rx1, near).wait_recv()
    for c in range(4):
        e_acc1[c] = (eb[b * 4 + c].astype(F32) + e_rx1[c].astype(F32)).astype(BF)
    for r in range(1, 4):
        send(2, r, e_acc1.at[g ^ r], e_rx2.at[r], cross[r])
    reduced(1, 0, sb.at[other], s_rx1, near).wait_recv()
    for c in range(4):
        s_acc1[c] = sb[b * 4 + c] + s_rx1[c]
    for r in range(1, 4):
        send(3, r, s_acc1.at[g ^ r], s_rx2.at[r], cross[r])
    grads(1, act_all, by_act)
    for r in range(1, 4):
        reduced(2, r, e_acc1.at[g ^ r], e_rx2.at[r], cross[r]).wait_recv()
    e_acc2[...] = (
        e_acc1[g].astype(F32) + e_rx2[1].astype(F32) + e_rx2[2].astype(F32) + e_rx2[3].astype(F32)
    ).astype(BF)
    rows_of = lambda i: pl.ds(pl.multiple_of(i * piece, piece), piece)
    for r in range(1, z_count):
        send(4, r, e_acc2.at[rows_of(z ^ r)], e_rx3.at[r], along[r])
    for r in range(1, 4):
        reduced(3, r, s_acc1.at[g ^ r], s_rx2.at[r], cross[r]).wait_recv()
    s_rx3[z] = s_acc1[g] + s_rx2[1] + s_rx2[2] + s_rx2[3]
    for r in range(1, z_count):
        send(5, r, s_rx3.at[z], s_rx3.at[z], along[r])
    total = e_acc2[rows_of(z), :].astype(F32)
    for r in range(1, z_count):
        reduced(4, r, e_acc2.at[rows_of(z ^ r)], e_rx3.at[r], along[r]).wait_recv()
        total = total + e_rx3[r].astype(F32)
    e_piece[...] = total.astype(BF)
    own = b * 4 + g
    cols_of = lambda i: pl.ds(pl.multiple_of(i * lanes, lanes), lanes)
    for r in range(1, z_count):
        send(6, r, e_piece, big_ref.at[rows_of(z), cols_of(own)], along[r])
    big_ref[rows_of(z), cols_of(own)] = total.astype(BF)
    for r in range(1, z_count):
        reduced(5, r, s_rx3.at[z], s_rx3.at[z ^ r], along[r]).wait_recv()
    s_total = s_rx3[0]
    for i in range(1, z_count):
        s_total = s_total + s_rx3[i]
    small_ref[own] = s_total
    for r in range(1, 4):
        send(7, r, small_ref.at[own], small_ref.at[own], cross[r])
    for r in range(1, z_count):
        reduced(6, r, e_piece, big_ref.at[rows_of(z ^ r), cols_of(own)], along[r]).wait_recv()
    for r in range(1, 4):
        send(8, r, big_ref.at[:, cols_of(own)], big_ref.at[:, cols_of(own)], cross[r])
    for r in range(1, 4):
        reduced(7, r, small_ref.at[own], small_ref.at[b * 4 + (g ^ r)], cross[r]).wait_recv()
    send(9, 0, small_ref.at[mine], small_ref.at[mine], near)
    send(10, 0, big_ref.at[:, cols_of(own)], big_ref.at[:, cols_of(own)], near)
    for r in range(1, 4):
        theirs = b * 4 + (g ^ r)
        reduced(8, r, big_ref.at[:, cols_of(own)], big_ref.at[:, cols_of(theirs)], cross[r]).wait_recv()
        send(10, r, big_ref.at[:, cols_of(theirs)], big_ref.at[:, cols_of(theirs)], near)

    def widen(i):
        embed_out[:, cols_of(i)] = big_ref[:, cols_of(i)].astype(F32)

    for r in range(4):
        widen(b * 4 + (g ^ r))
    reduced(9, 0, small_ref.at[mine], small_ref.at[other], near).wait_recv()
    for r in range(4):
        theirs = (1 - b) * 4 + (g ^ r)
        reduced(10, r, big_ref.at[:, cols_of(theirs)], big_ref.at[:, cols_of(theirs)], near).wait_recv()
        widen(theirs)
    for c in range(chunks):
        at = slice(c * lanes, (c + 1) * lanes)
        router_out[:, at] = small_ref[c, :experts]
        gain_out[:, at] = small_ref[c, experts : experts + 1]
        if c * 8 < stem:
            stem_out[c * 8 : c * 8 + 8] = small_ref[c, experts + 8 :]
    for copy in sent:
        copy.wait_send()
    for copy in strips:
        copy.wait_send()

    @pl.loop(0, count)
    def _(k):
        @pl.when(k > 0)
        def _():
            rows_moves[0](k).wait_send()
            cots_moves[0](k).wait_send()
            back(k).wait_send()

        for copy in rows_moves[1:] + cots_moves[1:] + (sum_near_a, sum_near_b, sum_far):
            copy(k).wait_send()

    for end in ends:
        end.wait()


def local(
    raw_tiles, stem_weight, embed_weight, norm_gain, router_weight, w_gate, w_up, w_down, routes,
    cotangent,
):
    tokens, width = cotangent.shape
    owners, members = lax.axis_size("de"), lax.axis_size("tp")
    experts = w_gate.shape[0] * owners
    cap = 2 * tokens // experts
    share = w_gate.shape[2]
    channels = raw_tiles.shape[0]
    stem = stem_weight.shape[0]
    patch_dim = embed_weight.shape[0]
    total = owners * members * cap
    shape = jax.ShapeDtypeStruct
    table = jnp.asarray(tap_table(channels), BF)
    taps = jnp.pad(stem_weight.reshape(stem, channels * 9), ((0, 0), (0, TAPS - channels * 9)))
    anywhere = pl.BlockSpec(memory_space=pl.ANY)
    lanes = width // 8
    z_count = owners // 2
    small_rows = experts + 16
    piece = patch_dim // z_count
    vmem, dma = pltpu.VMEM, pltpu.SemaphoreType.DMA
    mix, grad_embed, router_rows, grad_gain, taps_grad, grad_gate, grad_up, grad_down = pl.pallas_call(
        step_kernel,
        out_shape=(
            shape((tokens, width), BF),
            shape((patch_dim, width), F32),
            shape((experts, width), F32),
            shape((1, width), F32),
            shape((stem, lanes), F32),
            shape(w_gate.shape, F32),
            shape(w_up.shape, F32),
            shape(w_down.shape, F32),
        ),
        in_specs=[VMEM] * 6 + [anywhere] * 5,
        out_specs=(VMEM,) * 5 + (anywhere,) * 3,
        scratch_shapes=[
            vmem(table.shape, BF),
            vmem(embed_weight.shape, BF),
            vmem((width, share), BF),
            vmem((width, share), BF),
            vmem((share, width), BF),
            vmem((share, width), BF),
            vmem((share, width), BF),
            vmem((width, share), BF),
            vmem((2,) + raw_tiles.shape, BF),
            vmem((experts, cap, width + 128), BF),
            vmem((experts, cap, width), BF),
            vmem((owners, members, cap, width + 128), BF),
            vmem((owners, members, cap, width), BF),
            vmem((owners, members, 2 * cap, width), BF),
            vmem((owners, 2, 2 * cap, width), BF),
            vmem((owners, 2 * cap, width), BF),
            vmem((owners, 2 * cap, width), BF),
            vmem((total, width), BF),
            vmem((total, width), BF),
            vmem((total, share), BF),
            vmem((total, share), BF),
            vmem((total, share), BF),
            vmem((3, 2, 512, width // 2), F32),
            vmem((tokens, patch_dim), F32),
            vmem((tokens, patch_dim), BF),
            vmem((tokens, width), F32),
            vmem((tokens, 1), F32),
            vmem((tokens, width), BF),
            vmem((tokens, 1), F32),
            vmem((tokens, 1), jnp.int32),
            vmem((tokens, CLASSES * TAPS), BF),
            vmem((8, patch_dim, lanes), BF),
            vmem((4, patch_dim, lanes), BF),
            vmem((4, patch_dim, lanes), BF),
            vmem((4, patch_dim, lanes), BF),
            vmem((patch_dim, lanes), BF),
            vmem((z_count, piece, lanes), BF),
            vmem((piece, lanes), BF),
            vmem((8, small_rows, lanes), F32),
            vmem((4, small_rows, lanes), F32),
            vmem((4, small_rows, lanes), F32),
            vmem((4, small_rows, lanes), F32),
            vmem((z_count, small_rows, lanes), F32),
            vmem((patch_dim, width), BF),
            vmem((8, small_rows, lanes), F32),
            dma((5,)),
            dma,
            dma((3, 2)),
            dma((2,)),
            dma((2,)),
            dma((12, owners)),
            dma((12, owners)),
            dma((11, max(4, z_count))),
            dma((11, max(4, z_count))),
        ],
        compiler_params=pltpu.CompilerParams(
            vmem_limit_bytes=60 << 20, collective_id=1, has_side_effects=True
        ),
        name="step",
    )(
        raw_tiles, taps, norm_gain.reshape(1, width), router_weight, routes, cotangent,
        table, embed_weight, w_gate, w_up, w_down,
    )
    return (
        mix, grad_gate, grad_up, grad_down, router_rows.T, grad_gain.reshape(width), grad_embed,
        taps_grad[:, : channels * 9].reshape(stem_weight.shape),
    )


def solution(mesh):
    tiles = P(("de", "tp"), None)
    columns, rows = P("de", None, "tp"), P("de", "tp", None)
    return jax.shard_map(
        local,
        mesh=mesh,
        in_specs=(
            P(None, ("de", "tp"), None), P(), P(), P(), P(), columns, columns, rows, tiles, tiles,
        ),
        out_specs=(tiles, columns, columns, rows, P(), P(), P(), P()),
        check_vma=False,
    )
```
